256 devices in a mesh: patch: 64 (over x, z, core), epoch: 4 (over y).
Axes of the slice: x: 4, y: 4, z: 8, core: 2. Of those that a mesh axis runs over, the one named last changes fastest.
Arguments:
- images: bfloat16 [12288, 128, 128], P(('patch', 'epoch')), may hold values from -6 to 6
- variance: bfloat16 [12288, 128, 128], P(('patch', 'epoch')), may hold values from 0.25 to 4
- coefficients: float32 [12288, 3, 15], P(('patch', 'epoch')), may hold values from -1.8 to 1.8
- patch_of: int32 [12288, 1], P(('patch', 'epoch')), may hold values from 0 to 63; in each aligned block of 48 rows (0 to 47, 48 to 95, ...) at most 2 rows name the same one
- slot_of: int32 [12288], P(('patch', 'epoch')), may hold values from 0 to 15
Outputs:
- coadd: float32 [1024, 128, 128], P(('patch', 'epoch'))
- depth: float32 [1024, 128, 128], P(('patch', 'epoch'))
The draws below stay inside these ranges and needn't reach their ends.
Inputs may be any that keep to these rules, and one draw needn't show every extreme that they name: `patch_of`: among the rows of one device no patch is named more than 2 times; in some device's rows one patch is named exactly 2 times.
All inputs are finite; a program needn't handle non-finite values.
Results may differ from the reference program's by a relative error of at most 0.02.
Values may be sent and summed in bfloat16 or wider, within the bound.
No kernel may reach another device: no remote copies, remote signals or barrier semaphores. Data moves between devices by JAX's collectives and lax.ppermute only.
A program may use at most 128 MiB of HBM per device.

```python
import math
import jax
import jax.numpy as jnp
import numpy as np
from jax import lax

PIX = 128
BASES = 15
SLOTS = 16
BLK_DEV = 48
CAP = 2
TOTAL = 12288
TILES = 1024
N_PATCH = 64


def with_ends(array, rng, low, high):
    longest = array.shape.index(max(array.shape))
    spots = []
    for shift in (0, 1):
        where = [jax.random.randint(jax.random.fold_in(rng, axis), (), 0, length) for axis, length in enumerate(array.shape)]
        where[longest] = (where[longest] + shift) % array.shape[longest]
        spots.append(tuple(where))
    return array.at[spots[0]].set(low).at[spots[1]].set(high)


def levels(stream_key, extent, cuts, smallest, high):
    gain, own = 1.0, jax.random.fold_in(stream_key, 6)
    for axis_at, parts in cuts:
        steps = jnp.exp(jax.random.uniform(jax.random.fold_in(own, axis_at), (parts,), jnp.float32, smallest / len(cuts), high / len(cuts)))
        gain = gain * jnp.repeat(steps, extent[axis_at] // parts).reshape([-1 if axis == axis_at else 1 for axis in range(len(extent))])
    return gain


def assign_block(own_key, own, number, rows, amount, top, most, lean):
    order = jax.random.permutation(own_key, amount)
    packed, usual = shares(amount, rows * top, most, lean, True), shares(amount, rows * top, most, lean, False)
    places = jnp.arange(amount)

    def named(lengths, rotation):
        used = int((lengths > 0).sum())
        fixed = max(1, used // 4)
        moved = fixed + (places - fixed + rotation * (used - fixed)) % max(1, amount - fixed)
        return jnp.zeros((amount,), jnp.int32).at[order[jnp.where(places < fixed, places, moved)]].set(jnp.asarray(lengths, jnp.int32))

    lengths = jnp.where(number % 4 == 0, named(packed, number // 4), named(usual, number - number // 4 - 1))
    mixed = jax.random.permutation(jax.random.fold_in(own, 3), amount)
    donor, sink = mixed[0:amount // 2 * 2:2], mixed[1:amount // 2 * 2:2]
    room = jnp.minimum(lengths[donor] - 1, most - lengths[sink]) // 2
    room = jnp.where((donor == order[0]) | (sink == order[0]) | (lengths[sink] == 0), 0, jnp.maximum(room, 0))
    moved = jax.random.randint(jax.random.fold_in(own, 4), (amount // 2,), 0, 1 << 20) % (room + 1)
    lengths = lengths.at[donor].add(-moved).at[sink].add(moved)
    members = jnp.searchsorted(jnp.cumsum(lengths), jnp.arange(rows * top), side="right").astype(jnp.int32)
    grid = members.reshape(top, rows).T
    grid = grid[jax.random.permutation(jax.random.fold_in(own, 1), rows)]
    rotation = jax.random.randint(jax.random.fold_in(own, 2), (rows, 1), 0, top)
    return jnp.take_along_axis(grid, (jnp.arange(top)[None, :] + rotation) % top, axis=1)


def shares(count, total, limit, lean, full):
    loads = [(1 << 20) // math.isqrt(grade ** lean) + 1 for grade in range(1, count + 1)]
    largest = limit if full else min(limit, max(-(-total // count), total * loads[0] // sum(loads)))
    least = 1 if total - largest >= count - 1 else 0
    counts, surplus = [largest] + [least] * (count - 1), total - largest - least * (count - 1)
    while surplus > 0:
        movable = [i for i in range(1, count) if counts[i] < largest] or [i for i in range(1, count) if counts[i] < limit]
        pool, remaining = sum([loads[i] for i in movable]), surplus
        for i in movable:
            extra = min(limit - counts[i], max(1, remaining * loads[i] // pool), surplus)
            counts[i] = counts[i] + extra
            surplus = surplus - extra
    return np.array(counts)


def scatter_about(own_key, extent, scale, bound, split=(), kind=jnp.bfloat16):
    array = scale * jax.random.normal(own_key, extent, jnp.float32)
    if split:
        array = array * levels(own_key, extent, split, -0.22, 0.18)
    return jnp.clip(array, -bound, bound).astype(kind)


def setup_inputs(seed: int = 0) -> dict:
    key_of = jax.random.split(jax.random.key(seed), 6)
    images = scatter_about(key_of[0], (TOTAL, PIX, PIX), 1.0, 6.0, ((0, 256),))
    variance = jnp.clip(jnp.exp(math.log(4.0) - 2.7725887 * jax.random.uniform(key_of[1], (TOTAL, PIX, PIX), jnp.float32) ** levels(key_of[1], (TOTAL, PIX, PIX), ((0, 256),), -0.2, 0.2)), 0.25, 4.0).astype(jnp.bfloat16)
    coefficients = scatter_about(key_of[2], (TOTAL, 3, BASES), 0.3, 1.8, ((0, 256),), jnp.float32)
    patch_of_keys = jax.random.split(jax.random.fold_in(key_of[3], 1), TOTAL // BLK_DEV)
    patch_of_turns = jax.random.permutation(jax.random.fold_in(key_of[3], 3), TOTAL // BLK_DEV)
    patch_of = jax.vmap(lambda own, number: assign_block(jax.random.fold_in(key_of[3], 2), own, number, BLK_DEV, N_PATCH, 1, CAP, 2))(patch_of_keys, patch_of_turns).reshape((TOTAL, 1))
    slot_of = with_ends(jax.random.randint(key_of[4], (TOTAL,), 0, SLOTS), jax.random.fold_in(key_of[4], 1), 0, SLOTS - 1).astype(jnp.int32)
    return dict(images=images, variance=variance, coefficients=coefficients, patch_of=patch_of, slot_of=slot_of)


tap_reach = 10
basis_pairs = ((0, 0), (1, 0), (0, 1), (2, 0), (0, 2))

def band_matrix(side_len, spread, degree):
    offsets = jnp.arange(2 * tap_reach + 1, dtype=jnp.int32) - tap_reach
    scaled = offsets.astype(jnp.float32) / spread
    tap_values = jnp.exp(-0.5 * scaled * scaled) * scaled ** degree
    tap_values = tap_values / jnp.sqrt(jnp.sum(tap_values * tap_values))
    out_index = jnp.arange(side_len, dtype=jnp.int32)[:, None]
    in_index = jnp.arange(side_len, dtype=jnp.int32)[None, :]
    offset_of = in_index - out_index
    hot_taps = offset_of[:, :, None] == offsets[None, None, :]
    return lax.optimization_barrier(jnp.sum(jnp.where(hot_taps, tap_values[None, None, :], 0.0), axis=-1))

def basis_tables(side_len):
    x_list = []
    y_list = []
    for level in range(3):
        spread = 2.0 ** level
        bands = [band_matrix(side_len, spread, degree) for degree in range(3)]
        x_list = x_list + [band.T for band in bands]
        for pair in basis_pairs:
            y_list.append(bands[pair[1]])
    x_tables = jnp.concatenate(x_list, axis=1).astype(jnp.bfloat16)
    y_tables = jnp.stack(y_list, axis=0).astype(jnp.bfloat16)
    coords = jnp.arange(side_len, dtype=jnp.float32)
    u_coord = (2.0 * coords - (side_len - 1)) / (side_len - 1)
    return (x_tables, y_tables, u_coord)

def x_picks():
    return [level * 3 + pair[0] for level in range(3) for pair in basis_pairs]

def match_block(block_img, coef_in, x_tables, y_tables, u_coord):
    side_len = block_img.shape[-1]
    x_passed = jnp.dot(block_img, x_tables, preferred_element_type=jnp.float32).astype(jnp.bfloat16)
    x_passed = x_passed.reshape(side_len, 9, side_len)
    picked = jnp.stack([x_passed[:, index, :] for index in x_picks()], axis=0)
    smoothed = jnp.einsum('bkr,brc->bkc', y_tables.astype(jnp.float32), picked.astype(jnp.float32), precision=lax.Precision.HIGHEST)
    spatial = jnp.einsum('cb,bkj->ckj', coef_in, smoothed, precision=lax.Precision.HIGHEST)
    matched = spatial[0] + u_coord[None, :] * spatial[1] + u_coord[:, None] * spatial[2]
    return matched.astype(jnp.bfloat16)

def reference(images, variance, coefficients, patch_of, slot_of):
    side_len = images.shape[-1]
    x_tables, y_tables, u_coord = basis_tables(side_len)

    def match_one(pair_in):
        return match_block(pair_in[0], pair_in[1], x_tables, y_tables, u_coord)
    matched = lax.map(match_one, (images, coefficients), batch_size=64)
    weight = 1.0 / variance.astype(jnp.float32)
    tile_index = (patch_of[:, 0] * SLOTS + slot_of).astype(jnp.int32)
    weighted = (weight * matched.astype(jnp.float32)).reshape(images.shape[0], -1)
    numerator = jax.ops.segment_sum(weighted, tile_index, TILES)
    depth = jax.ops.segment_sum(weight.reshape(images.shape[0], -1), tile_index, TILES)
    coadd = numerator / jnp.maximum(depth, 1.0)
    return (coadd.reshape(TILES, side_len, side_len), depth.reshape(TILES, side_len, side_len))
```

```python
import numpy as np
import ml_dtypes
import jax
import jax.numpy as jnp
from jax import lax
from jax.experimental import pallas as pl
from jax.experimental.pallas import tpu as pltpu
from jax.sharding import Mesh, PartitionSpec as P

PIX = 128
SLOTS = 16
HELD = 48
REACH = 10
GROUPS = 16
CAP = 8
QUARTER = PIX // 4
ROWS = CAP * QUARTER
TILES_HELD = 64
STEP = 4


def band(spread, degree):
    t = np.arange(-REACH, REACH + 1)
    scaled = t.astype(np.float32) / np.float32(spread)
    taps = np.exp(np.float32(-0.5) * scaled * scaled) * scaled**degree
    taps = (taps / np.sqrt(np.sum(taps * taps))).astype(np.float32)
    out = np.zeros((PIX, PIX), np.float32)
    for k in range(PIX):
        for off, tap in zip(t, taps):
            if 0 <= k + off < PIX:
                out[k, k + off] = tap
    return out


def tables():
    bands = [band(2.0**s, d) for s in range(3) for d in range(3)]
    x_table = np.concatenate([b.T for b in bands], axis=1).astype(ml_dtypes.bfloat16)
    y_table = np.concatenate(bands, axis=1).astype(ml_dtypes.bfloat16)
    return x_table, y_table


def place_weights(patch_ref, slot_ref, var_ref, buf_ref, at_ref, weight, meta_f, meta, count, sems):
    for g in range(GROUPS):
        count[g] = 0
    meta_f[...] = jnp.zeros_like(meta_f)
    lane = lax.broadcasted_iota(jnp.int32, (16, PIX), 1)

    def copy(i, g, row):
        rows = pl.ds(pl.multiple_of(row * QUARTER, QUARTER), QUARTER)
        return pltpu.make_async_copy(weight.at[i], buf_ref.at[g, :, rows, :], sems.at[0])

    def one(i, carry):
        patch = patch_ref[i]
        x_at = patch // 16
        z_at = (patch // 2) % 8
        core = patch % 2
        g = (x_at * 2 + z_at % 2) * 2 + core
        row = count[g]
        count[g] = row + 1
        tile = (z_at // 2) * SLOTS + slot_ref[i]
        at_ref[i] = g * CAP + row
        weight[i] = (1.0 / var_ref[i].astype(jnp.float32)).astype(jnp.bfloat16).reshape(4, QUARTER, PIX)
        copy(i, g, row).start()
        mark = jnp.where(lane == row, (tile + 1).astype(jnp.float32), meta_f[g])
        meta_f[g] = jnp.where(lane == CAP, (row + 1).astype(jnp.float32), mark)
        return carry

    lax.fori_loop(0, HELD, one, 0)
    meta[...] = meta_f[...].astype(jnp.bfloat16)
    metas = [
        pltpu.make_async_copy(meta, buf_ref.at[:, q, pl.ds(ROWS, 16), :], sems.at[1 + q])
        for q in range(4)
    ]
    for m in metas:
        m.start()

    def drain(i, carry):
        copy(i, 0, 0).wait()
        return carry

    lax.fori_loop(0, HELD, drain, 0)
    for m in metas:
        m.wait()


def match_blocks(at_ref, coef_ref, img_ref, var_ref, xt_ref, yt_ref, buf_ref, z_ref, out_ref, sems):
    step = pl.program_id(0)
    last = pl.num_programs(0) - 1
    slot = lax.rem(step, 2)

    def copy(n, which, at):
        g = at // CAP
        row = at % CAP
        rows = pl.ds(pl.multiple_of(row * QUARTER, QUARTER), QUARTER)
        return pltpu.make_async_copy(out_ref.at[which, n], buf_ref.at[g, :, rows, :], sems.at[which])

    @pl.when(step >= 2)
    def _():
        for n in range(STEP):
            copy(n, slot, 0).wait()

    cols = lax.broadcasted_iota(jnp.int32, (1, PIX), 1).astype(jnp.float32)
    u = (2.0 * cols - (PIX - 1)) / (PIX - 1)
    rows = lax.broadcasted_iota(jnp.int32, (PIX, 1), 0).astype(jnp.float32)
    v = (2.0 * rows - (PIX - 1)) / (PIX - 1)
    for n in range(STEP):
        base = (step * STEP + n) * 45
        x_all = jnp.dot(img_ref[n], xt_ref[...], preferred_element_type=jnp.float32)

        def flat(b):
            return coef_ref[base + b] + coef_ref[base + 15 + b] * u

        def slope(b):
            return coef_ref[base + 30 + b]

        for s in range(3):
            b = 5 * s
            x0, x1, x2 = (x_all[:, (3 * s + d) * PIX : (3 * s + d + 1) * PIX] for d in range(3))
            parts = (
                (flat(b) * x0 + flat(b + 1) * x1 + flat(b + 3) * x2, slope(b) * x0 + slope(b + 1) * x1 + slope(b + 3) * x2),
                (flat(b + 2) * x0, slope(b + 2) * x0),
                (flat(b + 4) * x0, slope(b + 4) * x0),
            )
            for j in range(3):
                k = (3 * s + j) * PIX
                z_ref[n % 2, k : k + PIX, :PIX] = parts[j][0].astype(jnp.bfloat16)
                z_ref[n % 2, k : k + PIX, PIX:] = parts[j][1].astype(jnp.bfloat16)
        both = jnp.dot(yt_ref[...], z_ref[n % 2], preferred_element_type=jnp.float32)
        matched = both[:, :PIX] + v * both[:, PIX:]
        weighted = matched / var_ref[n].astype(jnp.float32)
        out_ref[slot, n] = weighted.astype(jnp.bfloat16).reshape(4, QUARTER, PIX)
    for n in range(STEP):
        copy(n, slot, at_ref[step * STEP + n]).start()

    @pl.when(step == last)
    def _():
        for which in (1 - slot, slot):
            for n in range(STEP):
                copy(n, which, 0).wait()


def sum_tiles(tile_ref, count_ref, got_ref, out_ref, total):
    step = pl.program_id(0)
    sources = got_ref.shape[0]

    @pl.when(step == 0)
    def _():
        total[...] = jnp.zeros_like(total)

    for n in range(sources):
        source = step * sources + n

        def add(row, carry):
            tile = tile_ref[source * CAP + row]
            rows = pl.ds(pl.multiple_of(row * QUARTER, QUARTER), QUARTER)
            total[tile] += got_ref[n, rows, :].astype(jnp.float32)
            return carry

        lax.fori_loop(0, count_ref[source], add, 0)

    @pl.when(step == pl.num_programs(0) - 1)
    def _():
        out_ref[...] = total[...].astype(jnp.bfloat16).reshape(out_ref.shape)


def tile_sums(tiles, counts, got):
    sources, rows, _ = got.shape
    each = 8
    return pl.pallas_call(
        sum_tiles,
        out_shape=jax.ShapeDtypeStruct((16, 4 * QUARTER, PIX), jnp.bfloat16),
        grid_spec=pltpu.PrefetchScalarGridSpec(
            num_scalar_prefetch=2,
            grid=(sources // each,),
            in_specs=[pl.BlockSpec((each, rows, PIX), lambda i, *_: (i, 0, 0))],
            out_specs=pl.BlockSpec((16, 4 * QUARTER, PIX), lambda i, *_: (0, 0, 0)),
            scratch_shapes=[pltpu.VMEM((TILES_HELD, QUARTER, PIX), jnp.float32)],
        ),
        compiler_params=pltpu.CompilerParams(vmem_limit_bytes=24 * 2**20),
        cost_estimate=pl.CostEstimate(flops=2 * 2**20, bytes_accessed=5 * 2**20, transcendentals=0),
    )(tiles, counts, got)


def local(images, variance, coefficients, patch_of, slot_of):
    x_table, y_table = tables()
    smem = pl.BlockSpec(memory_space=pltpu.SMEM)
    vmem = pl.BlockSpec(memory_space=pltpu.VMEM)
    anywhere = pl.BlockSpec(memory_space=pl.ANY)
    weight_buf, at = pl.pallas_call(
        place_weights,
        out_shape=(
            jax.ShapeDtypeStruct((GROUPS, 4, ROWS + 16, PIX), jnp.bfloat16),
            jax.ShapeDtypeStruct((HELD,), jnp.int32),
        ),
        in_specs=[smem, smem, vmem],
        out_specs=(anywhere, smem),
        scratch_shapes=[
            pltpu.VMEM((HELD, 4, QUARTER, PIX), jnp.bfloat16),
            pltpu.VMEM((GROUPS, 16, PIX), jnp.float32),
            pltpu.VMEM((GROUPS, 16, PIX), jnp.bfloat16),
            pltpu.SMEM((GROUPS,), jnp.int32),
            pltpu.SemaphoreType.DMA((5,)),
        ],
        compiler_params=pltpu.CompilerParams(vmem_limit_bytes=24 * 2**20),
    )(patch_of.reshape(HELD), slot_of, variance)
    group = ("x", "zl", "c", "y")
    weight_got = lax.all_to_all(
        weight_buf.reshape(64, ROWS + 16, PIX), group, split_axis=0, concat_axis=0, tiled=True
    )
    matched_buf = pl.pallas_call(
        match_blocks,
        out_shape=jax.ShapeDtypeStruct((GROUPS, 4, ROWS, PIX), jnp.bfloat16),
        grid_spec=pltpu.PrefetchScalarGridSpec(
            num_scalar_prefetch=2,
            grid=(HELD // STEP,),
            in_specs=[
                pl.BlockSpec((STEP, PIX, PIX), lambda i, *_: (i, 0, 0)),
                pl.BlockSpec((STEP, PIX, PIX), lambda i, *_: (i, 0, 0)),
                pl.BlockSpec((PIX, 9 * PIX), lambda i, *_: (0, 0)),
                pl.BlockSpec((PIX, 9 * PIX), lambda i, *_: (0, 0)),
            ],
            out_specs=anywhere,
            scratch_shapes=[
                pltpu.VMEM((2, 9 * PIX, 2 * PIX), jnp.bfloat16),
                pltpu.VMEM((2, STEP, 4, QUARTER, PIX), jnp.bfloat16),
                pltpu.SemaphoreType.DMA((2,)),
            ],
        ),
        compiler_params=pltpu.CompilerParams(vmem_limit_bytes=32 * 2**20),
        cost_estimate=pl.CostEstimate(flops=6 * 10**9, bytes_accessed=6 * 2**20, transcendentals=0),
    )(at, coefficients.reshape(-1), images, variance, jnp.asarray(x_table), jnp.asarray(y_table))
    matched_got = lax.all_to_all(
        matched_buf.reshape(64, ROWS, PIX), group, split_axis=0, concat_axis=0, tiled=True
    )
    meta = weight_got[:, ROWS, :16].astype(jnp.int32)
    tiles = (meta[:, :CAP] - 1).reshape(-1)
    counts = meta[:, CAP]
    depth_part = tile_sums(tiles, counts, weight_got)
    depth_got = lax.all_to_all(depth_part, ("zh", "y"), split_axis=0, concat_axis=0, tiled=True)
    num_part = tile_sums(tiles, counts, matched_got)
    num_got = lax.all_to_all(num_part, ("zh", "y"), split_axis=0, concat_axis=0, tiled=True)

    def whole(got):
        parts = got.reshape(4, 4, 4, QUARTER, PIX).astype(jnp.float32)
        return jnp.sum(parts, axis=0).transpose(1, 0, 2, 3).reshape(4, PIX, PIX)

    depth = whole(depth_got)
    return whole(num_got) / jnp.maximum(depth, 1.0), depth


def solution(mesh):
    names = ("x", "zh", "zl", "c", "y")
    fine = Mesh(mesh.devices.reshape(4, 4, 2, 2, 4), names)
    return jax.shard_map(
        local,
        mesh=fine,
        in_specs=(P(names, None, None), P(names, None, None), P(names, None, None), P(names, None), P(names)),
        out_specs=(P(names, None, None), P(names, None, None)),
        check_vma=False,
    )
```

```python
import numpy as np
import ml_dtypes
import jax
import jax.numpy as jnp
from jax import lax
from jax.experimental import pallas as pl
from jax.experimental.pallas import tpu as pltpu
from jax.sharding import Mesh, PartitionSpec as P

PIX = 128
SLOTS = 16
HELD = 48
REACH = 10
GROUP = 64
PARTS = 4
ROWS = PARTS * HELD
META = 16
ALL_BLOCKS = GROUP * HELD
TILES = 256
STEP = 4
LOADS = 4
PARAMS = pltpu.CompilerParams(vmem_limit_bytes=56 * 2**20)

VMEM_SPEC = pl.BlockSpec(memory_space=pltpu.VMEM)
HBM_SPEC = pl.BlockSpec(memory_space=pltpu.HBM)


def band(spread, degree):
    t = np.arange(-REACH, REACH + 1)
    scaled = t.astype(np.float32) / np.float32(spread)
    taps = np.exp(np.float32(-0.5) * scaled * scaled) * scaled**degree
    taps = (taps / np.sqrt(np.sum(taps * taps))).astype(np.float32)
    out = np.zeros((PIX, PIX), np.float32)
    for k in range(PIX):
        for off, tap in zip(t, taps):
            if 0 <= k + off < PIX:
                out[k, k + off] = tap
    return out


def tables():
    bands = [band(2.0**s, d) for s in range(3) for d in range(3)]
    x_table = np.concatenate([b.T for b in bands], axis=1).astype(ml_dtypes.bfloat16)
    y_table = np.concatenate(bands, axis=1).astype(ml_dtypes.bfloat16)
    return x_table, y_table


def match_blocks(coef_ref, img_ref, var_ref, xt_ref, yt_ref, meta_ref, out_hbm, z_ref, staged, packed, sems):
    step = pl.program_id(0)
    last = pl.num_programs(0) - 1

    def put(part, i, value):
        staged[pl.ds(part * HELD + i, GROUP, stride=ROWS), :] = value

    cols = lax.broadcasted_iota(jnp.int32, (1, PIX), 1).astype(jnp.float32)
    u = (2.0 * cols - (PIX - 1)) / (PIX - 1)
    rows = lax.broadcasted_iota(jnp.int32, (PIX, 1), 0).astype(jnp.float32)
    v = (2.0 * rows - (PIX - 1)) / (PIX - 1)
    for n in range(STEP):
        base = (step * STEP + n) * 45
        x_all = jnp.dot(img_ref[n], xt_ref[...], preferred_element_type=jnp.float32)

        def flat(b):
            return coef_ref[base + b] + coef_ref[base + 15 + b] * u

        def slope(b):
            return coef_ref[base + 30 + b]

        for s in range(3):
            b = 5 * s
            x0, x1, x2 = (x_all[:, (3 * s + d) * PIX : (3 * s + d + 1) * PIX] for d in range(3))
            parts = (
                (flat(b) * x0 + flat(b + 1) * x1 + flat(b + 3) * x2, slope(b) * x0 + slope(b + 1) * x1 + slope(b + 3) * x2),
                (flat(b + 2) * x0, slope(b + 2) * x0),
                (flat(b + 4) * x0, slope(b + 4) * x0),
            )
            for j in range(3):
                k = (3 * s + j) * PIX
                z_ref[n % 2, k : k + PIX, :PIX] = parts[j][0].astype(jnp.bfloat16)
                z_ref[n % 2, k : k + PIX, PIX:] = parts[j][1].astype(jnp.bfloat16)
        both = jnp.dot(yt_ref[...], z_ref[n % 2], preferred_element_type=jnp.float32)
        matched = both[:, :PIX] + v * both[:, PIX:]
        weight = 1.0 / var_ref[n].astype(jnp.float32)
        weighted = matched * weight
        i = step * STEP + n
        put(0, i, weight[:GROUP])
        put(1, i, weight[GROUP:])
        put(2, i, weighted[:GROUP])
        put(3, i, weighted[GROUP:])

    @pl.when(step == last)
    def _():
        copies = []
        each = GROUP // 8
        for k in range(8):
            for d in range(k * each, (k + 1) * each):
                packed[d, :ROWS, :] = staged[d * ROWS : (d + 1) * ROWS, :].astype(jnp.bfloat16)
                packed[d, ROWS:, :] = meta_ref[...]
            at = pl.ds(k * each, each)
            copies.append(pltpu.make_async_copy(packed.at[at], out_hbm.at[at], sems.at[k]))
            copies[-1].start()
        for c in copies:
            c.wait()


def sum_tiles(id_ref, got_hbm, *refs):
    outs, (blocks, hot, sems) = refs[:4], refs[4:]
    held = GROUP // LOADS
    loads = []
    for n in range(LOADS):
        at = pl.ds(n * held, held)
        for part in range(PARTS):
            src = got_hbm.at[at, pl.ds(part * HELD, HELD), :]
            dst = blocks.at[at, :, pl.ds(part * PIX, PIX)]
            loads.append(pltpu.make_async_copy(src, dst, sems.at[n * PARTS + part]))
    for c in loads:
        c.start()
    tile = lax.broadcasted_iota(jnp.int32, (TILES, PIX), 0)
    for m, out in enumerate(outs):
        for k in range(ALL_BLOCKS // PIX):
            ids = id_ref[k : k + 1, :]
            hot[:, k * PIX : (k + 1) * PIX] = jnp.where(ids == tile + m * TILES, 1.0, 0.0).astype(jnp.bfloat16)
        if m == 0:
            for c in loads:
                c.wait()
        values = blocks[...].reshape(ALL_BLOCKS, PARTS * PIX)
        out[...] = jnp.dot(hot[...], values, preferred_element_type=jnp.float32).astype(jnp.bfloat16)


def add_halves(a_ref, b_ref, c_ref, d_ref, out_ref, turned):
    total = sum(ref[...].astype(jnp.float32) for ref in (a_ref, b_ref, c_ref, d_ref))
    for part in range(PARTS):
        for s in range(4):
            turned[pl.ds(part * 4 + s, GROUP, stride=16), :] = total[s * GROUP : (s + 1) * GROUP, part * PIX : (part + 1) * PIX]
    out_ref[...] = turned[...].astype(jnp.bfloat16).reshape(GROUP, 16, PIX)


def combine(got_ref, coadd_ref, depth_ref, flat):
    flat[...] = got_ref[...].astype(jnp.float32).reshape(GROUP * 16, PIX)
    for s in range(4):
        for half in range(2):
            rows = slice(half * GROUP, (half + 1) * GROUP)
            depth = flat[pl.ds(half * 4 + s, GROUP, stride=16), :]
            num = flat[pl.ds((2 + half) * 4 + s, GROUP, stride=16), :]
            depth_ref[s, rows, :] = depth
            coadd_ref[s, rows, :] = num / jnp.maximum(depth, 1.0)


def local(images, variance, coefficients, patch_of, slot_of):
    x_table, y_table = tables()
    patch = patch_of.reshape(HELD)
    z_at = (patch // 2) % 8
    owner = ((patch // 16 * 2 + z_at % 2) * 2 + patch % 2) * 4 + slot_of // 4
    z_by = (z_at // 2 - lax.axis_index("zh")) % 4
    tile = jnp.pad((z_by * 4 + slot_of % 4) * GROUP + owner, (0, PIX - HELD))
    code = jnp.stack([tile % PIX, tile // PIX]).astype(jnp.bfloat16)
    meta = jnp.broadcast_to(code[:, None, :], (2, META // 2, PIX)).reshape(META, PIX)
    buf = pl.pallas_call(
        match_blocks,
        out_shape=jax.ShapeDtypeStruct((GROUP, ROWS + META, PIX), jnp.bfloat16),
        grid_spec=pltpu.PrefetchScalarGridSpec(
            num_scalar_prefetch=1,
            grid=(HELD // STEP,),
            in_specs=[
                pl.BlockSpec((STEP, PIX, PIX), lambda i, *_: (i, 0, 0)),
                pl.BlockSpec((STEP, PIX, PIX), lambda i, *_: (i, 0, 0)),
                pl.BlockSpec((PIX, 9 * PIX), lambda i, *_: (0, 0)),
                pl.BlockSpec((PIX, 9 * PIX), lambda i, *_: (0, 0)),
                pl.BlockSpec((META, PIX), lambda i, *_: (0, 0)),
            ],
            out_specs=HBM_SPEC,
            scratch_shapes=[
                pltpu.VMEM((2, 9 * PIX, 2 * PIX), jnp.bfloat16),
                pltpu.VMEM((GROUP * ROWS, PIX), jnp.float32),
                pltpu.VMEM((GROUP, ROWS + META, PIX), jnp.bfloat16),
                pltpu.SemaphoreType.DMA((8,)),
            ],
        ),
        compiler_params=PARAMS,
    )(coefficients.reshape(-1), images, variance, jnp.asarray(x_table), jnp.asarray(y_table), meta)
    group = ("x", "zl", "c", "y")
    got = lax.all_to_all(buf, group, split_axis=0, concat_axis=0, tiled=True)
    code = got[:, ROWS :: META // 2, :HELD].astype(jnp.int32)
    ids = (code[:, 0] + PIX * code[:, 1]).reshape(ALL_BLOCKS // PIX, PIX)
    part = jax.ShapeDtypeStruct((TILES, PARTS * PIX), jnp.bfloat16)
    parts = pl.pallas_call(
        sum_tiles,
        out_shape=[part] * 4,
        in_specs=[VMEM_SPEC, HBM_SPEC],
        out_specs=[VMEM_SPEC] * 4,
        scratch_shapes=[
            pltpu.VMEM((GROUP, HELD, PARTS * PIX), jnp.bfloat16),
            pltpu.VMEM((TILES, ALL_BLOCKS), jnp.bfloat16),
            pltpu.SemaphoreType.DMA((LOADS * PARTS,)),
        ],
        compiler_params=PARAMS,
    )(ids, got)
    moved = [lax.ppermute(parts[by], "zh", [(i, (i + by) % 4) for i in range(4)]) for by in (2, 1, 3)]
    summed = pl.pallas_call(
        add_halves,
        out_shape=jax.ShapeDtypeStruct((GROUP, 16, PIX), jnp.bfloat16),
        in_specs=[VMEM_SPEC] * 4,
        out_specs=VMEM_SPEC,
        scratch_shapes=[pltpu.VMEM((GROUP * 16, PIX), jnp.float32)],
        compiler_params=PARAMS,
    )(parts[0], *moved)
    whole = lax.all_to_all(summed, group, split_axis=0, concat_axis=0, tiled=True)
    out = jax.ShapeDtypeStruct((4, PIX, PIX), jnp.float32)
    return pl.pallas_call(
        combine,
        out_shape=(out, out),
        in_specs=[VMEM_SPEC],
        out_specs=(VMEM_SPEC, VMEM_SPEC),
        scratch_shapes=[pltpu.VMEM((GROUP * 16, PIX), jnp.float32)],
        compiler_params=PARAMS,
    )(whole)


def solution(mesh):
    names = ("x", "zh", "zl", "c", "y")
    fine = Mesh(mesh.devices.reshape(4, 4, 2, 2, 4), names)
    return jax.shard_map(
        local,
        mesh=fine,
        in_specs=(P(names, None, None), P(names, None, None), P(names, None, None), P(names, None), P(names)),
        out_specs=(P(names, None, None), P(names, None, None)),
        check_vma=False,
    )
```

```python
import functools

import numpy as np
import ml_dtypes
import jax
import jax.numpy as jnp
from jax import lax
from jax.experimental import pallas as pl
from jax.experimental.pallas import tpu as pltpu
from jax.sharding import Mesh, PartitionSpec as P

PIX = 128
SLOTS = 16
HELD = 48
REACH = 10
GROUP = 64
ROWS = 2 * HELD
META = 16
ALL_BLOCKS = GROUP * HELD
TILES = 256
BATCH = 16
STEP = 4
LOADS = 8
PARAMS = pltpu.CompilerParams(vmem_limit_bytes=56 * 2**20)

VMEM_SPEC = pl.BlockSpec(memory_space=pltpu.VMEM)
HBM_SPEC = pl.BlockSpec(memory_space=pltpu.HBM)


def band(spread, degree):
    t = np.arange(-REACH, REACH + 1)
    scaled = t.astype(np.float32) / np.float32(spread)
    taps = np.exp(np.float32(-0.5) * scaled * scaled) * scaled**degree
    taps = (taps / np.sqrt(np.sum(taps * taps))).astype(np.float32)
    out = np.zeros((PIX, PIX), np.float32)
    for k in range(PIX):
        for off, tap in zip(t, taps):
            if 0 <= k + off < PIX:
                out[k, k + off] = tap
    return out


def tables():
    bands = [band(2.0**s, d) for s in range(3) for d in range(3)]
    x_table = np.concatenate([b.T for b in bands], axis=1).astype(ml_dtypes.bfloat16)
    y_table = np.concatenate(bands, axis=1).astype(ml_dtypes.bfloat16)
    return x_table, y_table


def put(staged, i, value):
    for half in range(2):
        staged[pl.ds(half * HELD + i, GROUP, stride=ROWS), :] = value[half * GROUP : (half + 1) * GROUP]


def pack(staged, packed, out_hbm, sems):
    def group(n):
        copies = []
        for half in range(2):
            at = pl.ds(half * HELD + n * BATCH, BATCH)
            for d in range(GROUP):
                row = d * ROWS + half * HELD + n * BATCH
                packed[d, at, :] = staged[row : row + BATCH, :].astype(jnp.bfloat16)
            copies.append(pltpu.make_async_copy(packed.at[:, at, :], out_hbm.at[:, at, :], sems.at[2 * n + half]))
            copies[-1].start()
        return copies

    return group


def weigh_blocks(zh_ref, patch_hbm, slot_hbm, var_hbm, out_hbm, patch_ref, slot_ref, marks, var_ref, staged, packed, in_sems, sems):
    held = HELD // LOADS
    loads = []
    for n in range(LOADS):
        at = pl.ds(n * held, held)
        loads.append(pltpu.make_async_copy(var_hbm.at[at], var_ref.at[at], in_sems.at[n]))
    loads.append(pltpu.make_async_copy(patch_hbm, patch_ref, in_sems.at[LOADS]))
    loads.append(pltpu.make_async_copy(slot_hbm, slot_ref, in_sems.at[LOADS + 1]))
    for c in loads[-2:] + loads[:-2]:
        c.start()
    for c in loads[-2:]:
        c.wait()
    patch, slot = patch_ref[...], slot_ref[...]
    z_at = (patch // 2) % 8
    z_by = (z_at // 2 + 4 - zh_ref[0]) % 4
    owner = ((patch // 16 * 2 + z_at % 2) * 2 + patch % 2) * 4 + slot // 4
    tile = (z_by * 4 + slot % 4) * GROUP + owner
    low = lax.broadcasted_iota(jnp.int32, (META, HELD), 0) < META // 2
    marks[...] = jnp.zeros_like(marks)
    marks[:, :HELD] = jnp.where(low, tile % PIX, tile // PIX).astype(jnp.float32)
    meta = marks[...].astype(jnp.bfloat16)
    for d in range(GROUP):
        packed[d, ROWS:, :] = meta
    rows = pl.ds(ROWS, META)
    copies = [pltpu.make_async_copy(packed.at[:, rows, :], out_hbm.at[:, rows, :], sems.at[6])]
    copies[0].start()
    group = pack(staged, packed, out_hbm, sems)
    for n in range(LOADS):
        loads[n].wait()
        for i in range(n * held, (n + 1) * held):
            put(staged, i, 1.0 / var_ref[i].astype(jnp.float32))
            if i % BATCH == BATCH - 1:
                copies += group(i // BATCH)
    for c in copies:
        c.wait()


def match_blocks(coef_ref, img_ref, var_ref, xt_ref, yt_ref, out_hbm, z_ref, staged, packed, sems):
    step = pl.program_id(0)
    last = pl.num_programs(0) - 1

    cols = lax.broadcasted_iota(jnp.int32, (1, PIX), 1).astype(jnp.float32)
    u = (2.0 * cols - (PIX - 1)) / (PIX - 1)
    rows = lax.broadcasted_iota(jnp.int32, (PIX, 1), 0).astype(jnp.float32)
    v = (2.0 * rows - (PIX - 1)) / (PIX - 1)
    for n in range(STEP):
        base = (step * STEP + n) * 45
        x_all = jnp.dot(img_ref[n], xt_ref[...], preferred_element_type=jnp.float32)

        def flat(b):
            return coef_ref[base + b] + coef_ref[base + 15 + b] * u

        def slope(b):
            return coef_ref[base + 30 + b]

        for s in range(3):
            b = 5 * s
            x0, x1, x2 = (x_all[:, (3 * s + d) * PIX : (3 * s + d + 1) * PIX] for d in range(3))
            parts = (
                (flat(b) * x0 + flat(b + 1) * x1 + flat(b + 3) * x2, slope(b) * x0 + slope(b + 1) * x1 + slope(b + 3) * x2),
                (flat(b + 2) * x0, slope(b + 2) * x0),
                (flat(b + 4) * x0, slope(b + 4) * x0),
            )
            for j in range(3):
                k = (3 * s + j) * PIX
                z_ref[n % 2, k : k + PIX, :PIX] = parts[j][0].astype(jnp.bfloat16)
                z_ref[n % 2, k : k + PIX, PIX:] = parts[j][1].astype(jnp.bfloat16)
        both = jnp.dot(yt_ref[...], z_ref[n % 2], preferred_element_type=jnp.float32)
        matched = both[:, :PIX] + v * both[:, PIX:]
        put(staged, step * STEP + n, matched / var_ref[n].astype(jnp.float32))

    group = pack(staged, packed, out_hbm, sems)
    each = BATCH // STEP
    for n in range(HELD // BATCH):

        @pl.when(step == (n + 1) * each - 1)
        def _():
            group(n)

    @pl.when(step == last)
    def _():
        for n in range(HELD // BATCH):
            for half in range(2):
                at = pl.ds(half * HELD + n * BATCH, BATCH)
                pltpu.make_async_copy(packed.at[:, at, :], out_hbm.at[:, at, :], sems.at[2 * n + half]).wait()


def sum_tiles(halves, id_ref, got_hbm, *refs):
    outs, (blocks, hot, sems) = refs[-3 - len(halves) : -3], refs[-3:]
    held = GROUP // LOADS
    loads = []
    for n in range(LOADS):
        at = pl.ds(n * held, held)
        for half in range(2):
            src = got_hbm.at[at, pl.ds(half * HELD, HELD), :]
            dst = blocks.at[at, :, pl.ds(half * PIX, PIX)]
            loads.append(pltpu.make_async_copy(src, dst, sems.at[2 * n + half]))
    for c in loads:
        c.start()
    tile = lax.broadcasted_iota(jnp.int32, (TILES, PIX), 0)
    for n, (m, out) in enumerate(zip(halves, outs)):
        for k in range(ALL_BLOCKS // PIX):
            ids = id_ref[k : k + 1, :]
            hot[:, k * PIX : (k + 1) * PIX] = jnp.where(ids == tile + m * TILES, 1.0, 0.0).astype(jnp.bfloat16)
        if n == 0:
            for c in loads:
                c.wait()
        values = blocks[...].reshape(ALL_BLOCKS, 2 * PIX)
        out[...] = jnp.dot(hot[...], values, preferred_element_type=jnp.float32).astype(jnp.bfloat16)


def tile_sums(ids, got, halves, after=()):
    part = jax.ShapeDtypeStruct((TILES, 2 * PIX), jnp.bfloat16)
    return pl.pallas_call(
        functools.partial(sum_tiles, halves),
        out_shape=[part] * len(halves),
        in_specs=[VMEM_SPEC, HBM_SPEC] + [pl.BlockSpec(memory_space=pl.ANY)] * len(after),
        out_specs=[VMEM_SPEC] * len(halves),
        scratch_shapes=[
            pltpu.VMEM((GROUP, HELD, 2 * PIX), jnp.bfloat16),
            pltpu.VMEM((TILES, ALL_BLOCKS), jnp.bfloat16),
            pltpu.SemaphoreType.DMA((LOADS * 2,)),
        ],
        compiler_params=PARAMS,
    )(ids, got, *after)


def over_z(part, by):
    return lax.ppermute(part, "zh", [(i, (i + by) % 4) for i in range(4)])


def add_halves(a_ref, b_ref, c_ref, d_ref, out_ref):
    out_ref[...] = sum(ref[...].astype(jnp.float32) for ref in (a_ref, b_ref, c_ref, d_ref))


def add_all(depth_ref, a_ref, b_ref, c_ref, d_ref, out_ref, turned):
    num = sum(ref[...].astype(jnp.float32) for ref in (a_ref, b_ref, c_ref, d_ref))
    for n, total in enumerate((depth_ref[...], num)):
        for half in range(2):
            for s in range(4):
                at = pl.ds((2 * n + half) * 4 + s, GROUP, stride=16)
                turned[at, :] = total[s * GROUP : (s + 1) * GROUP, half * PIX : (half + 1) * PIX]
    out_ref[...] = turned[...].astype(jnp.bfloat16).reshape(GROUP, 16, PIX)


def combine(got_ref, coadd_ref, depth_ref, flat):
    flat[...] = got_ref[...].astype(jnp.float32).reshape(GROUP * 16, PIX)
    for s in range(4):
        for half in range(2):
            rows = slice(half * GROUP, (half + 1) * GROUP)
            depth = flat[pl.ds(half * 4 + s, GROUP, stride=16), :]
            num = flat[pl.ds((2 + half) * 4 + s, GROUP, stride=16), :]
            depth_ref[s, rows, :] = depth
            coadd_ref[s, rows, :] = num / jnp.maximum(depth, 1.0)


def local(images, variance, coefficients, patch_of, slot_of):
    x_table, y_table = tables()
    scratch = [pltpu.VMEM((GROUP * ROWS, PIX), jnp.float32)]
    weight_buf = pl.pallas_call(
        weigh_blocks,
        out_shape=jax.ShapeDtypeStruct((GROUP, ROWS + META, PIX), jnp.bfloat16),
        in_specs=[pl.BlockSpec(memory_space=pltpu.SMEM)] + [HBM_SPEC] * 3,
        out_specs=HBM_SPEC,
        scratch_shapes=[
            pltpu.VMEM((1, HELD), jnp.int32),
            pltpu.VMEM((1, HELD), jnp.int32),
            pltpu.VMEM((META, PIX), jnp.float32),
            pltpu.VMEM((HELD, PIX, PIX), jnp.bfloat16),
        ]
        + scratch
        + [
            pltpu.VMEM((GROUP, ROWS + META, PIX), jnp.bfloat16),
            pltpu.SemaphoreType.DMA((LOADS + 2,)),
            pltpu.SemaphoreType.DMA((7,)),
        ],
        compiler_params=PARAMS,
    )(lax.axis_index("zh").reshape(1), patch_of.reshape(1, HELD), slot_of.reshape(1, HELD), variance)
    group = ("x", "zl", "c", "y")
    weight_got = lax.all_to_all(weight_buf, group, split_axis=0, concat_axis=0, tiled=True)
    matched_buf = pl.pallas_call(
        match_blocks,
        out_shape=jax.ShapeDtypeStruct((GROUP, ROWS, PIX), jnp.bfloat16),
        grid_spec=pltpu.PrefetchScalarGridSpec(
            num_scalar_prefetch=1,
            grid=(HELD // STEP,),
            in_specs=[
                pl.BlockSpec((STEP, PIX, PIX), lambda i, *_: (i, 0, 0)),
                pl.BlockSpec((STEP, PIX, PIX), lambda i, *_: (i, 0, 0)),
                pl.BlockSpec((PIX, 9 * PIX), lambda i, *_: (0, 0)),
                pl.BlockSpec((PIX, 9 * PIX), lambda i, *_: (0, 0)),
            ],
            out_specs=HBM_SPEC,
            scratch_shapes=[pltpu.VMEM((2, 9 * PIX, 2 * PIX), jnp.bfloat16)]
            + scratch
            + [pltpu.VMEM((GROUP, ROWS, PIX), jnp.bfloat16), pltpu.SemaphoreType.DMA((LOADS,))],
        ),
        compiler_params=PARAMS,
        cost_estimate=pl.CostEstimate(flops=6 * 10**9, bytes_accessed=6 * 2**20, transcendentals=0),
    )(coefficients.reshape(-1), images, variance, jnp.asarray(x_table), jnp.asarray(y_table))
    matched_got = lax.all_to_all(matched_buf, group, split_axis=0, concat_axis=0, tiled=True)
    code = weight_got[:, ROWS :: META // 2, :HELD].astype(jnp.int32)
    ids = (code[:, 0] + PIX * code[:, 1]).reshape(ALL_BLOCKS // PIX, PIX)
    weight_parts = tile_sums(ids, weight_got, (0, 1, 2, 3))
    depth = pl.pallas_call(
        add_halves,
        out_shape=jax.ShapeDtypeStruct((TILES, 2 * PIX), jnp.float32),
        in_specs=[VMEM_SPEC] * 4,
        out_specs=VMEM_SPEC,
        compiler_params=PARAMS,
    )(weight_parts[0], *(over_z(weight_parts[by], by) for by in (2, 1, 3)))
    own, up, far, down = tile_sums(ids, matched_got, (0, 1, 2, 3), (weight_parts[0],))
    summed = pl.pallas_call(
        add_all,
        out_shape=jax.ShapeDtypeStruct((GROUP, 16, PIX), jnp.bfloat16),
        in_specs=[VMEM_SPEC] * 5,
        out_specs=VMEM_SPEC,
        scratch_shapes=[pltpu.VMEM((GROUP * 16, PIX), jnp.float32)],
        compiler_params=PARAMS,
    )(depth, own, over_z(far, 2), over_z(up, 1), over_z(down, 3))
    whole = lax.all_to_all(summed, group, split_axis=0, concat_axis=0, tiled=True)
    out = jax.ShapeDtypeStruct((4, PIX, PIX), jnp.float32)
    return pl.pallas_call(
        combine,
        out_shape=(out, out),
        in_specs=[VMEM_SPEC],
        out_specs=(VMEM_SPEC, VMEM_SPEC),
        scratch_shapes=[pltpu.VMEM((GROUP * 16, PIX), jnp.float32)],
        compiler_params=PARAMS,
    )(whole)


def solution(mesh):
    names = ("x", "zh", "zl", "c", "y")
    fine = Mesh(mesh.devices.reshape(4, 4, 2, 2, 4), names)
    return jax.shard_map(
        local,
        mesh=fine,
        in_specs=(P(names, None, None), P(names, None, None), P(names, None, None), P(names, None), P(names)),
        out_specs=(P(names, None, None), P(names, None, None)),
        check_vma=False,
    )
```

```python
import functools

import numpy as np
import ml_dtypes
import jax
import jax.numpy as jnp
from jax import lax
from jax.experimental import pallas as pl
from jax.experimental.pallas import tpu as pltpu
from jax.sharding import Mesh, PartitionSpec as P

PIX = 128
SLOTS = 16
HELD = 48
REACH = 10
GROUP = 64
ROWS = 2 * HELD
META = 16
ALL_BLOCKS = GROUP * HELD
TILES = 256
BATCH = 16
STEP = 4
LOADS = 8
PARAMS = pltpu.CompilerParams(vmem_limit_bytes=56 * 2**20)
SUM_PARAMS = pltpu.CompilerParams(vmem_limit_bytes=24 * 2**20)
ADD_PARAMS = pltpu.CompilerParams(vmem_limit_bytes=8 * 2**20)

VMEM_SPEC = pl.BlockSpec(memory_space=pltpu.VMEM)
HBM_SPEC = pl.BlockSpec(memory_space=pltpu.HBM)
ANY_SPEC = pl.BlockSpec(memory_space=pl.ANY)


def band(spread, degree):
    t = np.arange(-REACH, REACH + 1)
    scaled = t.astype(np.float32) / np.float32(spread)
    taps = np.exp(np.float32(-0.5) * scaled * scaled) * scaled**degree
    taps = (taps / np.sqrt(np.sum(taps * taps))).astype(np.float32)
    out = np.zeros((PIX, PIX), np.float32)
    for k in range(PIX):
        for off, tap in zip(t, taps):
            if 0 <= k + off < PIX:
                out[k, k + off] = tap
    return out


def tables():
    bands = [band(2.0**s, d) for s in range(3) for d in range(3)]
    x_table = np.concatenate([b.T for b in bands], axis=1).astype(ml_dtypes.bfloat16)
    y_table = np.concatenate(bands, axis=1).astype(ml_dtypes.bfloat16)
    return x_table, y_table


def put(staged, i, value):
    for half in range(2):
        staged[pl.ds(half * HELD + i, GROUP, stride=ROWS), :] = value[half * GROUP : (half + 1) * GROUP]


def pack(staged, packed, out_hbm, sems):
    def group(n):
        copies = []
        for half in range(2):
            at = pl.ds(half * HELD + n * BATCH, BATCH)
            for d in range(GROUP):
                row = d * ROWS + half * HELD + n * BATCH
                packed[d, at, :] = staged[row : row + BATCH, :].astype(jnp.bfloat16)
            copies.append(pltpu.make_async_copy(packed.at[:, at, :], out_hbm.at[:, at, :], sems.at[2 * n + half]))
            copies[-1].start()
        return copies

    return group


def weigh_blocks(zh_ref, patch_hbm, slot_hbm, var_hbm, out_hbm, patch_ref, slot_ref, marks, var_ref, staged, packed, in_sems, sems):
    held = HELD // LOADS
    loads = []
    for n in range(LOADS):
        at = pl.ds(n * held, held)
        loads.append(pltpu.make_async_copy(var_hbm.at[at], var_ref.at[at], in_sems.at[n]))
    loads.append(pltpu.make_async_copy(patch_hbm, patch_ref, in_sems.at[LOADS]))
    loads.append(pltpu.make_async_copy(slot_hbm, slot_ref, in_sems.at[LOADS + 1]))
    for c in loads[-2:] + loads[:-2]:
        c.start()
    for c in loads[-2:]:
        c.wait()
    patch, slot = patch_ref[...], slot_ref[...]
    z_at = (patch // 2) % 8
    z_by = (z_at // 2 + 4 - zh_ref[0]) % 4
    owner = ((patch // 16 * 2 + z_at % 2) * 2 + patch % 2) * 4 + slot // 4
    tile = (z_by * 4 + slot % 4) * GROUP + owner
    low = lax.broadcasted_iota(jnp.int32, (META, HELD), 0) < META // 2
    marks[...] = jnp.zeros_like(marks)
    marks[:, :HELD] = jnp.where(low, tile % PIX, tile // PIX).astype(jnp.float32)
    meta = marks[...].astype(jnp.bfloat16)
    for d in range(GROUP):
        packed[d, ROWS:, :] = meta
    rows = pl.ds(ROWS, META)
    copies = [pltpu.make_async_copy(packed.at[:, rows, :], out_hbm.at[:, rows, :], sems.at[6])]
    copies[0].start()
    group = pack(staged, packed, out_hbm, sems)
    for n in range(LOADS):
        loads[n].wait()
        for i in range(n * held, (n + 1) * held):
            put(staged, i, pl.reciprocal(var_ref[i].astype(jnp.float32), approx=True))
            if i % BATCH == BATCH - 1:
                copies += group(i // BATCH)
    for c in copies:
        c.wait()


def match_blocks(coef_ref, img_ref, var_ref, xt_ref, yt_ref, out_hbm, z_ref, staged, packed, sems):
    step = pl.program_id(0)
    last = pl.num_programs(0) - 1

    cols = lax.broadcasted_iota(jnp.int32, (1, PIX), 1).astype(jnp.float32)
    u = (2.0 * cols - (PIX - 1)) / (PIX - 1)
    rows = lax.broadcasted_iota(jnp.int32, (PIX, 1), 0).astype(jnp.float32)
    v = (2.0 * rows - (PIX - 1)) / (PIX - 1)
    for n in range(STEP):
        base = (step * STEP + n) * 45
        x_all = jnp.dot(img_ref[n], xt_ref[...], preferred_element_type=jnp.float32)

        def flat(b):
            return coef_ref[base + b] + coef_ref[base + 15 + b] * u

        def slope(b):
            return coef_ref[base + 30 + b]

        for s in range(3):
            b = 5 * s
            x0, x1, x2 = (x_all[:, (3 * s + d) * PIX : (3 * s + d + 1) * PIX] for d in range(3))
            parts = (
                (flat(b) * x0 + flat(b + 1) * x1 + flat(b + 3) * x2, slope(b) * x0 + slope(b + 1) * x1 + slope(b + 3) * x2),
                (flat(b + 2) * x0, slope(b + 2) * x0),
                (flat(b + 4) * x0, slope(b + 4) * x0),
            )
            for j in range(3):
                k = (3 * s + j) * PIX
                z_ref[n % 2, k : k + PIX, :PIX] = parts[j][0].astype(jnp.bfloat16)
                z_ref[n % 2, k : k + PIX, PIX:] = parts[j][1].astype(jnp.bfloat16)
        both = jnp.dot(yt_ref[...], z_ref[n % 2], preferred_element_type=jnp.float32)
        matched = both[:, :PIX] + v * both[:, PIX:]
        put(staged, step * STEP + n, matched / var_ref[n].astype(jnp.float32))

    group = pack(staged, packed, out_hbm, sems)
    each = BATCH // STEP
    for n in range(HELD // BATCH):

        @pl.when(step == (n + 1) * each - 1)
        def _():
            group(n)

    @pl.when(step == last)
    def _():
        for n in range(HELD // BATCH):
            for half in range(2):
                at = pl.ds(half * HELD + n * BATCH, BATCH)
                pltpu.make_async_copy(packed.at[:, at, :], out_hbm.at[:, at, :], sems.at[2 * n + half]).wait()


def read_marks(got_ref, table, id_ref):
    code = got_ref[:, ROWS:, :].astype(jnp.float32)
    lane = lax.broadcasted_iota(jnp.int32, (GROUP, PIX), 1)
    tile = code[:, 0, :] + PIX * code[:, META // 2, :]
    table[...] = jnp.where(lane < HELD, tile, 0.0).astype(jnp.int32)
    lane = lax.broadcasted_iota(jnp.int32, (8, PIX), 1)
    rows = [jnp.zeros((8, PIX), jnp.int32)] * 4
    for n in range(8):
        row, at = n * HELD // PIX, n * HELD % PIX
        moved = pltpu.roll(table[pl.ds(n, 8, stride=8), :], at, 1) if at else table[pl.ds(n, 8, stride=8), :]
        rows[row] = rows[row] + jnp.where(lane >= at, moved, 0)
        rows[row + 1] = rows[row + 1] + jnp.where(lane < at, moved, 0)
    for row in range(3):
        id_ref[pl.ds(row, 8, stride=3), :] = rows[row]


def sum_blocks(id_ref, got_ref, outs, hot):
    tile = lax.broadcasted_iota(jnp.int32, (4 * TILES, PIX), 0)
    for k in range(ALL_BLOCKS // PIX):
        hot[:, k * PIX : (k + 1) * PIX] = jnp.where(id_ref[k : k + 1, :] == tile, 1.0, 0.0).astype(jnp.bfloat16)
    halves = [got_ref[:, half * HELD : (half + 1) * HELD, :].reshape(ALL_BLOCKS, PIX) for half in range(2)]
    total = jnp.dot(hot[...], jnp.concatenate(halves, axis=1), preferred_element_type=jnp.float32).astype(jnp.bfloat16)
    for m, out in enumerate(outs):
        out[...] = total[m * TILES : (m + 1) * TILES]


def sum_weights(got_ref, id_ref, *refs):
    read_marks(got_ref, refs[5], id_ref)
    sum_blocks(id_ref, got_ref, refs[:4], refs[4])


def sum_matched(id_ref, got_ref, *refs):
    sum_blocks(id_ref, got_ref, refs[:4], refs[4])


def tile_sums(got, ids=None):
    part = jax.ShapeDtypeStruct((TILES, 2 * PIX), jnp.bfloat16)
    hot = pltpu.VMEM((4 * TILES, ALL_BLOCKS), jnp.bfloat16)
    if ids is not None:
        return pl.pallas_call(
            sum_matched,
            out_shape=[part] * 4,
            in_specs=[VMEM_SPEC] * 2,
            out_specs=[VMEM_SPEC] * 4,
            scratch_shapes=[hot],
            compiler_params=SUM_PARAMS,
        )(ids, got)
    return pl.pallas_call(
        sum_weights,
        out_shape=[jax.ShapeDtypeStruct((ALL_BLOCKS // PIX, PIX), jnp.int32)] + [part] * 4,
        in_specs=[VMEM_SPEC],
        out_specs=[VMEM_SPEC] * 5,
        scratch_shapes=[hot, pltpu.VMEM((GROUP, PIX), jnp.int32)],
        compiler_params=SUM_PARAMS,
    )(got)


def over_z(part, by):
    return lax.ppermute(part, "zh", [(i, (i + by) % 4) for i in range(4)])


def add_halves(a_ref, b_ref, c_ref, d_ref, out_ref):
    out_ref[...] = sum(ref[...].astype(jnp.float32) for ref in (a_ref, b_ref, c_ref, d_ref))


def add_all(depth_ref, a_ref, b_ref, c_ref, d_ref, out_ref, turned):
    num = sum(ref[...].astype(jnp.float32) for ref in (a_ref, b_ref, c_ref, d_ref))
    for n, total in enumerate((depth_ref[...], num)):
        for half in range(2):
            for s in range(4):
                at = pl.ds((2 * n + half) * 4 + s, GROUP, stride=16)
                turned[at, :] = total[s * GROUP : (s + 1) * GROUP, half * PIX : (half + 1) * PIX]
    out_ref[...] = turned[...].astype(jnp.bfloat16).reshape(GROUP, 16, PIX)


def combine(got_ref, coadd_ref, depth_ref, flat):
    flat[...] = got_ref[...].astype(jnp.float32).reshape(GROUP * 16, PIX)
    for s in range(4):
        for half in range(2):
            rows = slice(half * GROUP, (half + 1) * GROUP)
            depth = flat[pl.ds(half * 4 + s, GROUP, stride=16), :]
            num = flat[pl.ds((2 + half) * 4 + s, GROUP, stride=16), :]
            depth_ref[s, rows, :] = depth
            coadd_ref[s, rows, :] = num / jnp.maximum(depth, 1.0)


def local(images, variance, coefficients, patch_of, slot_of):
    x_table, y_table = tables()
    scratch = [pltpu.VMEM((GROUP * ROWS, PIX), jnp.float32)]
    weight_buf = pl.pallas_call(
        weigh_blocks,
        out_shape=jax.ShapeDtypeStruct((GROUP, ROWS + META, PIX), jnp.bfloat16),
        in_specs=[pl.BlockSpec(memory_space=pltpu.SMEM)] + [HBM_SPEC] * 3,
        out_specs=HBM_SPEC,
        scratch_shapes=[
            pltpu.VMEM((1, HELD), jnp.int32),
            pltpu.VMEM((1, HELD), jnp.int32),
            pltpu.VMEM((META, PIX), jnp.float32),
            pltpu.VMEM((HELD, PIX, PIX), jnp.bfloat16),
        ]
        + scratch
        + [
            pltpu.VMEM((GROUP, ROWS + META, PIX), jnp.bfloat16),
            pltpu.SemaphoreType.DMA((LOADS + 2,)),
            pltpu.SemaphoreType.DMA((7,)),
        ],
        compiler_params=PARAMS,
    )(lax.axis_index("zh").reshape(1), patch_of.reshape(1, HELD), slot_of.reshape(1, HELD), variance)
    group = ("x", "zl", "c", "y")
    weight_got = lax.all_to_all(weight_buf, group, split_axis=0, concat_axis=0, tiled=True)
    matched_buf = pl.pallas_call(
        match_blocks,
        out_shape=jax.ShapeDtypeStruct((GROUP, ROWS, PIX), jnp.bfloat16),
        grid_spec=pltpu.PrefetchScalarGridSpec(
            num_scalar_prefetch=1,
            grid=(HELD // STEP,),
            in_specs=[
                pl.BlockSpec((STEP, PIX, PIX), lambda i, *_: (i, 0, 0)),
                pl.BlockSpec((STEP, PIX, PIX), lambda i, *_: (i, 0, 0)),
                pl.BlockSpec((PIX, 9 * PIX), lambda i, *_: (0, 0)),
                pl.BlockSpec((PIX, 9 * PIX), lambda i, *_: (0, 0)),
            ],
            out_specs=HBM_SPEC,
            scratch_shapes=[pltpu.VMEM((2, 9 * PIX, 2 * PIX), jnp.bfloat16)]
            + scratch
            + [pltpu.VMEM((GROUP, ROWS, PIX), jnp.bfloat16), pltpu.SemaphoreType.DMA((LOADS,))],
        ),
        compiler_params=PARAMS,
        cost_estimate=pl.CostEstimate(flops=6 * 10**9, bytes_accessed=6 * 2**20, transcendentals=0),
    )(coefficients.reshape(-1), images, variance, jnp.asarray(x_table), jnp.asarray(y_table))
    matched_got = lax.all_to_all(matched_buf, group, split_axis=0, concat_axis=0, tiled=True)
    ids, *weight_parts = tile_sums(weight_got)
    depth = pl.pallas_call(
        add_halves,
        out_shape=jax.ShapeDtypeStruct((TILES, 2 * PIX), jnp.float32),
        in_specs=[VMEM_SPEC] * 4,
        out_specs=VMEM_SPEC,
        compiler_params=ADD_PARAMS,
    )(weight_parts[0], *(over_z(weight_parts[by], by) for by in (2, 1, 3)))
    own, up, far, down = tile_sums(matched_got, ids)
    summed = pl.pallas_call(
        add_all,
        out_shape=jax.ShapeDtypeStruct((GROUP, 16, PIX), jnp.bfloat16),
        in_specs=[VMEM_SPEC] * 5,
        out_specs=VMEM_SPEC,
        scratch_shapes=[pltpu.VMEM((GROUP * 16, PIX), jnp.float32)],
        compiler_params=ADD_PARAMS,
    )(depth, own, over_z(far, 2), over_z(up, 1), over_z(down, 3))
    whole = lax.all_to_all(summed, group, split_axis=0, concat_axis=0, tiled=True)
    out = jax.ShapeDtypeStruct((4, PIX, PIX), jnp.float32)
    return pl.pallas_call(
        combine,
        out_shape=(out, out),
        in_specs=[VMEM_SPEC],
        out_specs=(VMEM_SPEC, VMEM_SPEC),
        scratch_shapes=[pltpu.VMEM((GROUP * 16, PIX), jnp.float32)],
        compiler_params=ADD_PARAMS,
    )(whole)


def solution(mesh):
    names = ("x", "zh", "zl", "c", "y")
    fine = Mesh(mesh.devices.reshape(4, 4, 2, 2, 4), names)
    return jax.shard_map(
        local,
        mesh=fine,
        in_specs=(P(names, None, None), P(names, None, None), P(names, None, None), P(names, None), P(names)),
        out_specs=(P(names, None, None), P(names, None, None)),
        check_vma=False,
    )
```

```python
import functools

import numpy as np
import ml_dtypes
import jax
import jax.numpy as jnp
from jax import lax
from jax.experimental import pallas as pl
from jax.experimental.pallas import tpu as pltpu
from jax.sharding import Mesh, PartitionSpec as P

PIX = 128
SLOTS = 16
HELD = 48
REACH = 10
GROUP = 64
ROWS = 2 * HELD
META = 16
ALL_BLOCKS = GROUP * HELD
TILES = 256
BATCH = 16
STRIDE = 40
STEP = 4
LOADS = 8
PARAMS = pltpu.CompilerParams(vmem_limit_bytes=56 * 2**20)
SUM_PARAMS = pltpu.CompilerParams(vmem_limit_bytes=24 * 2**20)
ADD_PARAMS = pltpu.CompilerParams(vmem_limit_bytes=8 * 2**20)

VMEM_SPEC = pl.BlockSpec(memory_space=pltpu.VMEM)
HBM_SPEC = pl.BlockSpec(memory_space=pltpu.HBM)
ANY_SPEC = pl.BlockSpec(memory_space=pl.ANY)


def band(spread, degree):
    t = np.arange(-REACH, REACH + 1)
    scaled = t.astype(np.float32) / np.float32(spread)
    taps = np.exp(np.float32(-0.5) * scaled * scaled) * scaled**degree
    taps = (taps / np.sqrt(np.sum(taps * taps))).astype(np.float32)
    out = np.zeros((PIX, PIX), np.float32)
    for k in range(PIX):
        for off, tap in zip(t, taps):
            if 0 <= k + off < PIX:
                out[k, k + off] = tap
    return out


def tables():
    bands = [band(2.0**s, d) for s in range(3) for d in range(3)]
    x_table = np.concatenate([b.T for b in bands], axis=1).astype(ml_dtypes.bfloat16)
    y_table = np.concatenate(bands, axis=1).astype(ml_dtypes.bfloat16)
    return x_table, y_table


def put(staged, i, value):
    for half in range(2):
        staged[pl.ds(half * BATCH + i % BATCH, GROUP, stride=STRIDE), :] = value[half * GROUP : (half + 1) * GROUP]


def pack(staged, packed, out_hbm, sems, n):
    copies = []
    for half in range(2):
        at = pl.ds(n * BATCH + half * HELD, BATCH)
        for d in range(GROUP):
            row = d * STRIDE + half * BATCH
            packed[d, at, :] = staged[row : row + BATCH, :].astype(jnp.bfloat16)
        copies.append(pltpu.make_async_copy(packed.at[:, at, :], out_hbm.at[:, at, :], sems.at[2 * n + half]))
        copies[-1].start()
    return copies


def weigh_blocks(zh_ref, patch_hbm, slot_hbm, var_hbm, out_hbm, patch_ref, slot_ref, marks, var_ref, packed, in_sems, sems, *staged):
    held = HELD // LOADS
    loads = []
    for n in range(LOADS):
        at = pl.ds(n * held, held)
        loads.append(pltpu.make_async_copy(var_hbm.at[at], var_ref.at[at], in_sems.at[n]))
    loads.append(pltpu.make_async_copy(patch_hbm, patch_ref, in_sems.at[LOADS]))
    loads.append(pltpu.make_async_copy(slot_hbm, slot_ref, in_sems.at[LOADS + 1]))
    for c in loads[-2:] + loads[:-2]:
        c.start()
    for c in loads[-2:]:
        c.wait()
    patch, slot = patch_ref[...], slot_ref[...]
    z_at = (patch // 2) % 8
    z_by = (z_at // 2 + 4 - zh_ref[0]) % 4
    owner = ((patch // 16 * 2 + z_at % 2) * 2 + patch % 2) * 4 + slot // 4
    tile = (z_by * 4 + slot % 4) * GROUP + owner
    low = lax.broadcasted_iota(jnp.int32, (META, HELD), 0) < META // 2
    marks[...] = jnp.zeros_like(marks)
    marks[:, :HELD] = jnp.where(low, tile % PIX, tile // PIX).astype(jnp.float32)
    meta = marks[...].astype(jnp.bfloat16)
    for d in range(GROUP):
        packed[d, ROWS:, :] = meta
    rows = pl.ds(ROWS, META)
    copies = [pltpu.make_async_copy(packed.at[:, rows, :], out_hbm.at[:, rows, :], sems.at[6])]
    copies[0].start()
    for n in range(LOADS):
        loads[n].wait()
        for i in range(n * held, (n + 1) * held):
            put(staged[i // BATCH], i, pl.reciprocal(var_ref[i].astype(jnp.float32), approx=True))
            if i % BATCH == BATCH - 1:
                copies += pack(staged[i // BATCH], packed, out_hbm, sems, i // BATCH)
    for c in copies:
        c.wait()


def match_blocks(coef_ref, img_ref, var_ref, xt_ref, yt_ref, out_hbm, z_ref, staged, packed, sems):
    step = pl.program_id(0)
    last = pl.num_programs(0) - 1

    cols = lax.broadcasted_iota(jnp.int32, (1, PIX), 1).astype(jnp.float32)
    u = (2.0 * cols - (PIX - 1)) / (PIX - 1)
    rows = lax.broadcasted_iota(jnp.int32, (PIX, 1), 0).astype(jnp.float32)
    v = (2.0 * rows - (PIX - 1)) / (PIX - 1)
    for n in range(STEP):
        base = (step * STEP + n) * 45
        x_all = jnp.dot(img_ref[n], xt_ref[...], preferred_element_type=jnp.float32)

        def flat(b):
            return coef_ref[base + b] + coef_ref[base + 15 + b] * u

        def slope(b):
            return coef_ref[base + 30 + b]

        for s in range(3):
            b = 5 * s
            x0, x1, x2 = (x_all[:, (3 * s + d) * PIX : (3 * s + d + 1) * PIX] for d in range(3))
            parts = (
                (flat(b) * x0 + flat(b + 1) * x1 + flat(b + 3) * x2, slope(b) * x0 + slope(b + 1) * x1 + slope(b + 3) * x2),
                (flat(b + 2) * x0, slope(b + 2) * x0),
                (flat(b + 4) * x0, slope(b + 4) * x0),
            )
            for j in range(3):
                k = (3 * s + j) * PIX
                z_ref[n % 2, k : k + PIX, :PIX] = parts[j][0].astype(jnp.bfloat16)
                z_ref[n % 2, k : k + PIX, PIX:] = parts[j][1].astype(jnp.bfloat16)
        both = jnp.dot(yt_ref[...], z_ref[n % 2], preferred_element_type=jnp.float32)
        matched = both[:, :PIX] + v * both[:, PIX:]
        put(staged, step * STEP + n, matched / var_ref[n].astype(jnp.float32))

    each = BATCH // STEP
    for n in range(HELD // BATCH):

        @pl.when(step == (n + 1) * each - 1)
        def _():
            pack(staged, packed, out_hbm, sems, n)

    @pl.when(step == last)
    def _():
        for n in range(HELD // BATCH):
            for half in range(2):
                at = pl.ds(half * HELD + n * BATCH, BATCH)
                pltpu.make_async_copy(packed.at[:, at, :], out_hbm.at[:, at, :], sems.at[2 * n + half]).wait()


def read_marks(got_ref, table, id_ref):
    code = got_ref[:, ROWS:, :].astype(jnp.float32)
    lane = lax.broadcasted_iota(jnp.int32, (GROUP, PIX), 1)
    tile = code[:, 0, :] + PIX * code[:, META // 2, :]
    table[...] = jnp.where(lane < HELD, tile, 0.0).astype(jnp.int32)
    lane = lax.broadcasted_iota(jnp.int32, (8, PIX), 1)
    rows = [jnp.zeros((8, PIX), jnp.int32)] * 4
    for n in range(8):
        row, at = n * HELD // PIX, n * HELD % PIX
        moved = pltpu.roll(table[pl.ds(n, 8, stride=8), :], at, 1) if at else table[pl.ds(n, 8, stride=8), :]
        rows[row] = rows[row] + jnp.where(lane >= at, moved, 0)
        rows[row + 1] = rows[row + 1] + jnp.where(lane < at, moved, 0)
    for row in range(3):
        id_ref[pl.ds(row, 8, stride=3), :] = rows[row]


def sum_blocks(id_ref, got_ref, outs, hot):
    tile = lax.broadcasted_iota(jnp.int32, (4 * TILES, PIX), 0)
    for k in range(ALL_BLOCKS // PIX):
        hot[:, k * PIX : (k + 1) * PIX] = jnp.where(id_ref[k : k + 1, :] == tile, 1.0, 0.0).astype(jnp.bfloat16)
    halves = [got_ref[:, half * HELD : (half + 1) * HELD, :].reshape(ALL_BLOCKS, PIX) for half in range(2)]
    total = jnp.dot(hot[...], jnp.concatenate(halves, axis=1), preferred_element_type=jnp.float32).astype(jnp.bfloat16)
    for m, out in enumerate(outs):
        out[...] = total[m * TILES : (m + 1) * TILES]


def sum_weights(got_ref, id_ref, *refs):
    read_marks(got_ref, refs[5], id_ref)
    sum_blocks(id_ref, got_ref, refs[:4], refs[4])


def sum_matched(id_ref, got_ref, *refs):
    sum_blocks(id_ref, got_ref, refs[:4], refs[4])


def tile_sums(got, ids=None):
    part = jax.ShapeDtypeStruct((TILES, 2 * PIX), jnp.bfloat16)
    hot = pltpu.VMEM((4 * TILES, ALL_BLOCKS), jnp.bfloat16)
    if ids is not None:
        return pl.pallas_call(
            sum_matched,
            out_shape=[part] * 4,
            in_specs=[VMEM_SPEC] * 2,
            out_specs=[VMEM_SPEC] * 4,
            scratch_shapes=[hot],
            compiler_params=SUM_PARAMS,
        )(ids, got)
    return pl.pallas_call(
        sum_weights,
        out_shape=[jax.ShapeDtypeStruct((ALL_BLOCKS // PIX, PIX), jnp.int32)] + [part] * 4,
        in_specs=[VMEM_SPEC],
        out_specs=[VMEM_SPEC] * 5,
        scratch_shapes=[hot, pltpu.VMEM((GROUP, PIX), jnp.int32)],
        compiler_params=SUM_PARAMS,
    )(got)


def over_z(part, by):
    return lax.ppermute(part, "zh", [(i, (i + by) % 4) for i in range(4)])


def add_halves(a_ref, b_ref, c_ref, d_ref, out_ref):
    out_ref[...] = sum(ref[...].astype(jnp.float32) for ref in (a_ref, b_ref, c_ref, d_ref))


def add_all(depth_ref, a_ref, b_ref, c_ref, d_ref, out_ref, turned):
    num = sum(ref[...].astype(jnp.float32) for ref in (a_ref, b_ref, c_ref, d_ref))
    for n, total in enumerate((depth_ref[...], num)):
        for half in range(2):
            for s in range(4):
                at = pl.ds((2 * n + half) * 4 + s, GROUP, stride=16)
                turned[at, :] = total[s * GROUP : (s + 1) * GROUP, half * PIX : (half + 1) * PIX]
    out_ref[...] = turned[...].astype(jnp.bfloat16).reshape(GROUP, 16, PIX)


def combine(got_ref, coadd_ref, depth_ref, flat):
    flat[...] = got_ref[...].astype(jnp.float32).reshape(GROUP * 16, PIX)
    for s in range(4):
        for half in range(2):
            rows = slice(half * GROUP, (half + 1) * GROUP)
            depth = flat[pl.ds(half * 4 + s, GROUP, stride=16), :]
            num = flat[pl.ds((2 + half) * 4 + s, GROUP, stride=16), :]
            depth_ref[s, rows, :] = depth
            coadd_ref[s, rows, :] = num / jnp.maximum(depth, 1.0)


def local(images, variance, coefficients, patch_of, slot_of):
    x_table, y_table = tables()
    scratch = [pltpu.VMEM((GROUP * STRIDE, PIX), jnp.float32)]
    weight_buf = pl.pallas_call(
        weigh_blocks,
        out_shape=jax.ShapeDtypeStruct((GROUP, ROWS + META, PIX), jnp.bfloat16),
        in_specs=[pl.BlockSpec(memory_space=pltpu.SMEM)] + [HBM_SPEC] * 3,
        out_specs=HBM_SPEC,
        scratch_shapes=[
            pltpu.VMEM((1, HELD), jnp.int32),
            pltpu.VMEM((1, HELD), jnp.int32),
            pltpu.VMEM((META, PIX), jnp.float32),
            pltpu.VMEM((HELD, PIX, PIX), jnp.bfloat16),
            pltpu.VMEM((GROUP, ROWS + META, PIX), jnp.bfloat16),
            pltpu.SemaphoreType.DMA((LOADS + 2,)),
            pltpu.SemaphoreType.DMA((7,)),
        ]
        + scratch * (HELD // BATCH),
        compiler_params=PARAMS,
    )(lax.axis_index("zh").reshape(1), patch_of.reshape(1, HELD), slot_of.reshape(1, HELD), variance)
    group = ("x", "zl", "c", "y")
    weight_got = lax.all_to_all(weight_buf, group, split_axis=0, concat_axis=0, tiled=True)
    matched_buf = pl.pallas_call(
        match_blocks,
        out_shape=jax.ShapeDtypeStruct((GROUP, ROWS, PIX), jnp.bfloat16),
        grid_spec=pltpu.PrefetchScalarGridSpec(
            num_scalar_prefetch=1,
            grid=(HELD // STEP,),
            in_specs=[
                pl.BlockSpec((STEP, PIX, PIX), lambda i, *_: (i, 0, 0)),
                pl.BlockSpec((STEP, PIX, PIX), lambda i, *_: (i, 0, 0)),
                pl.BlockSpec((PIX, 9 * PIX), lambda i, *_: (0, 0)),
                pl.BlockSpec((PIX, 9 * PIX), lambda i, *_: (0, 0)),
            ],
            out_specs=HBM_SPEC,
            scratch_shapes=[pltpu.VMEM((2, 9 * PIX, 2 * PIX), jnp.bfloat16)]
            + scratch
            + [pltpu.VMEM((GROUP, ROWS, PIX), jnp.bfloat16), pltpu.SemaphoreType.DMA((LOADS,))],
        ),
        compiler_params=PARAMS,
        cost_estimate=pl.CostEstimate(flops=6 * 10**9, bytes_accessed=6 * 2**20, transcendentals=0),
    )(coefficients.reshape(-1), images, variance, jnp.asarray(x_table), jnp.asarray(y_table))
    matched_got = lax.all_to_all(matched_buf, group, split_axis=0, concat_axis=0, tiled=True)
    ids, *weight_parts = tile_sums(weight_got)
    depth = pl.pallas_call(
        add_halves,
        out_shape=jax.ShapeDtypeStruct((TILES, 2 * PIX), jnp.float32),
        in_specs=[VMEM_SPEC] * 4,
        out_specs=VMEM_SPEC,
        compiler_params=ADD_PARAMS,
    )(weight_parts[0], *(over_z(weight_parts[by], by) for by in (2, 1, 3)))
    own, up, far, down = tile_sums(matched_got, ids)
    summed = pl.pallas_call(
        add_all,
        out_shape=jax.ShapeDtypeStruct((GROUP, 16, PIX), jnp.bfloat16),
        in_specs=[VMEM_SPEC] * 5,
        out_specs=VMEM_SPEC,
        scratch_shapes=[pltpu.VMEM((GROUP * 16, PIX), jnp.float32)],
        compiler_params=ADD_PARAMS,
    )(depth, own, over_z(far, 2), over_z(up, 1), over_z(down, 3))
    whole = lax.all_to_all(summed, group, split_axis=0, concat_axis=0, tiled=True)
    out = jax.ShapeDtypeStruct((4, PIX, PIX), jnp.float32)
    return pl.pallas_call(
        combine,
        out_shape=(out, out),
        in_specs=[VMEM_SPEC],
        out_specs=(VMEM_SPEC, VMEM_SPEC),
        scratch_shapes=[pltpu.VMEM((GROUP * 16, PIX), jnp.float32)],
        compiler_params=ADD_PARAMS,
    )(whole)


def solution(mesh):
    names = ("x", "zh", "zl", "c", "y")
    fine = Mesh(mesh.devices.reshape(4, 4, 2, 2, 4), names)
    return jax.shard_map(
        local,
        mesh=fine,
        in_specs=(P(names, None, None), P(names, None, None), P(names, None, None), P(names, None), P(names)),
        out_specs=(P(names, None, None), P(names, None, None)),
        check_vma=False,
    )
```

```python
import functools

import numpy as np
import ml_dtypes
import jax
import jax.numpy as jnp
from jax import lax
from jax.experimental import pallas as pl
from jax.experimental.pallas import tpu as pltpu
from jax.sharding import Mesh, PartitionSpec as P

PIX = 128
SLOTS = 16
HELD = 48
REACH = 10
GROUP = 64
ROWS = 2 * HELD
META = 16
ALL_BLOCKS = GROUP * HELD
TILES = 256
BATCH = 16
TURN = 24
STRIDE = 40
STEP = 4
LOADS = 8
PARAMS = pltpu.CompilerParams(vmem_limit_bytes=56 * 2**20)
SUM_PARAMS = pltpu.CompilerParams(vmem_limit_bytes=24 * 2**20)
ADD_PARAMS = pltpu.CompilerParams(vmem_limit_bytes=8 * 2**20)

VMEM_SPEC = pl.BlockSpec(memory_space=pltpu.VMEM)
HBM_SPEC = pl.BlockSpec(memory_space=pltpu.HBM)
ANY_SPEC = pl.BlockSpec(memory_space=pl.ANY)


def band(spread, degree):
    t = np.arange(-REACH, REACH + 1)
    scaled = t.astype(np.float32) / np.float32(spread)
    taps = np.exp(np.float32(-0.5) * scaled * scaled) * scaled**degree
    taps = (taps / np.sqrt(np.sum(taps * taps))).astype(np.float32)
    out = np.zeros((PIX, PIX), np.float32)
    for k in range(PIX):
        for off, tap in zip(t, taps):
            if 0 <= k + off < PIX:
                out[k, k + off] = tap
    return out


def tables():
    bands = [band(2.0**s, d) for s in range(3) for d in range(3)]
    x_table = np.concatenate([b.T for b in bands], axis=1).astype(ml_dtypes.bfloat16)
    y_table = np.concatenate(bands, axis=1).astype(ml_dtypes.bfloat16)
    return x_table, y_table


def put(staged, i, value):
    for half in range(2):
        staged[pl.ds(half * BATCH + i % BATCH, GROUP, stride=STRIDE), :] = value[half * GROUP : (half + 1) * GROUP]


def pack(staged, packed, out_hbm, sems, n):
    copies = []
    for half in range(2):
        at = pl.ds(n * BATCH + half * HELD, BATCH)
        for d in range(GROUP):
            row = d * STRIDE + half * BATCH
            packed[d, at, :] = staged[row : row + BATCH, :].astype(jnp.bfloat16)
        copies.append(pltpu.make_async_copy(packed.at[:, at, :], out_hbm.at[:, at, :], sems.at[2 * n + half]))
        copies[-1].start()
    return copies


def weigh_blocks(zh_ref, patch_hbm, slot_hbm, var_hbm, out_hbm, patch_ref, slot_ref, marks, var_ref, packed, in_sems, sems, *staged):
    held = HELD // LOADS
    loads = []
    for n in range(LOADS):
        at = pl.ds(n * held, held)
        loads.append(pltpu.make_async_copy(var_hbm.at[at], var_ref.at[at], in_sems.at[n]))
    loads.append(pltpu.make_async_copy(patch_hbm, patch_ref, in_sems.at[LOADS]))
    loads.append(pltpu.make_async_copy(slot_hbm, slot_ref, in_sems.at[LOADS + 1]))
    for c in loads[-2:] + loads[:-2]:
        c.start()
    for c in loads[-2:]:
        c.wait()
    patch, slot = patch_ref[...], slot_ref[...]
    z_at = (patch // 2) % 8
    z_by = (z_at // 2 + 4 - zh_ref[0]) % 4
    owner = ((z_at % 2 * 2 + patch % 2) * 4 + patch // 16) * 4 + slot // 4
    tile = (z_by * 4 + slot % 4) * GROUP + owner
    low = lax.broadcasted_iota(jnp.int32, (META, HELD), 0) < META // 2
    marks[...] = jnp.zeros_like(marks)
    marks[:, :HELD] = jnp.where(low, tile % PIX, tile // PIX).astype(jnp.float32)
    meta = marks[...].astype(jnp.bfloat16)
    for d in range(GROUP):
        packed[d, ROWS:, :] = meta
    rows = pl.ds(ROWS, META)
    copies = [pltpu.make_async_copy(packed.at[:, rows, :], out_hbm.at[:, rows, :], sems.at[6])]
    copies[0].start()
    for n in range(LOADS):
        loads[n].wait()
        for i in range(n * held, (n + 1) * held):
            put(staged[i // BATCH], i, pl.reciprocal(var_ref[i].astype(jnp.float32), approx=True))
            if i % BATCH == BATCH - 1:
                copies += pack(staged[i // BATCH], packed, out_hbm, sems, i // BATCH)
    for c in copies:
        c.wait()


def match_blocks(coef_ref, img_ref, var_ref, xt_ref, yt_ref, out_hbm, z_ref, staged, packed, sems):
    step = pl.program_id(0)
    last = pl.num_programs(0) - 1

    cols = lax.broadcasted_iota(jnp.int32, (1, PIX), 1).astype(jnp.float32)
    u = (2.0 * cols - (PIX - 1)) / (PIX - 1)
    rows = lax.broadcasted_iota(jnp.int32, (PIX, 1), 0).astype(jnp.float32)
    v = (2.0 * rows - (PIX - 1)) / (PIX - 1)
    for n in range(STEP):
        base = (step * STEP + n) * 45
        x_all = jnp.dot(img_ref[n], xt_ref[...], preferred_element_type=jnp.float32)

        def flat(b):
            return coef_ref[base + b] + coef_ref[base + 15 + b] * u

        def slope(b):
            return coef_ref[base + 30 + b]

        for s in range(3):
            b = 5 * s
            x0, x1, x2 = (x_all[:, (3 * s + d) * PIX : (3 * s + d + 1) * PIX] for d in range(3))
            parts = (
                (flat(b) * x0 + flat(b + 1) * x1 + flat(b + 3) * x2, slope(b) * x0 + slope(b + 1) * x1 + slope(b + 3) * x2),
                (flat(b + 2) * x0, slope(b + 2) * x0),
                (flat(b + 4) * x0, slope(b + 4) * x0),
            )
            for j in range(3):
                k = (3 * s + j) * PIX
                z_ref[n % 2, k : k + PIX, :PIX] = parts[j][0].astype(jnp.bfloat16)
                z_ref[n % 2, k : k + PIX, PIX:] = parts[j][1].astype(jnp.bfloat16)
        both = jnp.dot(yt_ref[...], z_ref[n % 2], preferred_element_type=jnp.float32)
        matched = both[:, :PIX] + v * both[:, PIX:]
        put(staged, step * STEP + n, matched / var_ref[n].astype(jnp.float32))

    each = BATCH // STEP
    for n in range(HELD // BATCH):

        @pl.when(step == (n + 1) * each - 1)
        def _():
            pack(staged, packed, out_hbm, sems, n)

    @pl.when(step == last)
    def _():
        for n in range(HELD // BATCH):
            for half in range(2):
                at = pl.ds(half * HELD + n * BATCH, BATCH)
                pltpu.make_async_copy(packed.at[:, at, :], out_hbm.at[:, at, :], sems.at[2 * n + half]).wait()


def read_marks(got_ref, table, id_ref):
    code = got_ref[:, ROWS:, :].astype(jnp.float32)
    lane = lax.broadcasted_iota(jnp.int32, (GROUP, PIX), 1)
    tile = code[:, 0, :] + PIX * code[:, META // 2, :]
    table[...] = jnp.where(lane < HELD, tile, 0.0).astype(jnp.int32)
    lane = lax.broadcasted_iota(jnp.int32, (8, PIX), 1)
    rows = [jnp.zeros((8, PIX), jnp.int32)] * 4
    for n in range(8):
        row, at = n * HELD // PIX, n * HELD % PIX
        moved = pltpu.roll(table[pl.ds(n, 8, stride=8), :], at, 1) if at else table[pl.ds(n, 8, stride=8), :]
        rows[row] = rows[row] + jnp.where(lane >= at, moved, 0)
        rows[row + 1] = rows[row + 1] + jnp.where(lane < at, moved, 0)
    for row in range(3):
        id_ref[pl.ds(row, 8, stride=3), :] = rows[row]


def sum_blocks(id_ref, got_ref, outs, hot):
    tile = lax.broadcasted_iota(jnp.int32, (4 * TILES, PIX), 0)
    for k in range(ALL_BLOCKS // PIX):
        hot[:, k * PIX : (k + 1) * PIX] = jnp.where(id_ref[k : k + 1, :] == tile, 1.0, 0.0).astype(jnp.bfloat16)
    halves = [got_ref[:, half * HELD : (half + 1) * HELD, :].reshape(ALL_BLOCKS, PIX) for half in range(2)]
    total = jnp.dot(hot[...], jnp.concatenate(halves, axis=1), preferred_element_type=jnp.float32).astype(jnp.bfloat16)
    for m, out in enumerate(outs):
        out[...] = total[m * TILES : (m + 1) * TILES]


def sum_weights(got_ref, id_ref, *refs):
    read_marks(got_ref, refs[5], id_ref)
    sum_blocks(id_ref, got_ref, refs[:4], refs[4])


def sum_matched(id_ref, got_ref, *refs):
    sum_blocks(id_ref, got_ref, refs[:4], refs[4])


def tile_sums(got, ids=None):
    part = jax.ShapeDtypeStruct((TILES, 2 * PIX), jnp.bfloat16)
    hot = pltpu.VMEM((4 * TILES, ALL_BLOCKS), jnp.bfloat16)
    if ids is not None:
        return pl.pallas_call(
            sum_matched,
            out_shape=[part] * 4,
            in_specs=[VMEM_SPEC] * 2,
            out_specs=[VMEM_SPEC] * 4,
            scratch_shapes=[hot],
            compiler_params=SUM_PARAMS,
        )(ids, got)
    return pl.pallas_call(
        sum_weights,
        out_shape=[jax.ShapeDtypeStruct((ALL_BLOCKS // PIX, PIX), jnp.int32)] + [part] * 4,
        in_specs=[VMEM_SPEC],
        out_specs=[VMEM_SPEC] * 5,
        scratch_shapes=[hot, pltpu.VMEM((GROUP, PIX), jnp.int32)],
        compiler_params=SUM_PARAMS,
    )(got)


def over_z(part, by):
    return lax.ppermute(part, "zh", [(i, (i + by) % 4) for i in range(4)])


def add_halves(a_ref, b_ref, c_ref, d_ref, out_ref):
    out_ref[...] = sum(ref[...].astype(jnp.float32) for ref in (a_ref, b_ref, c_ref, d_ref))


def add_all(depth_ref, a_ref, b_ref, c_ref, d_ref, out_ref, turned):
    num = sum(ref[...].astype(jnp.float32) for ref in (a_ref, b_ref, c_ref, d_ref))
    for n, total in enumerate((depth_ref[...], num)):
        for half in range(2):
            for s in range(4):
                at = pl.ds((2 * n + half) * 4 + s, GROUP, stride=TURN)
                turned[at, :] = total[s * GROUP : (s + 1) * GROUP, half * PIX : (half + 1) * PIX]
    for d in range(GROUP):
        out_ref[d] = turned[d * TURN : d * TURN + 16, :].astype(jnp.bfloat16)


def combine(got_ref, coadd_ref, depth_ref, flat):
    for d in range(GROUP):
        flat[d * TURN : d * TURN + 16, :] = got_ref[d].astype(jnp.float32)
    for s in range(4):
        for half in range(2):
            rows = slice(half * GROUP, (half + 1) * GROUP)
            depth = flat[pl.ds(half * 4 + s, GROUP, stride=TURN), :]
            num = flat[pl.ds((2 + half) * 4 + s, GROUP, stride=TURN), :]
            depth_ref[s, rows, :] = depth
            coadd_ref[s, rows, :] = num / jnp.maximum(depth, 1.0)


def local(images, variance, coefficients, patch_of, slot_of):
    x_table, y_table = tables()
    scratch = [pltpu.VMEM((GROUP * STRIDE, PIX), jnp.float32)]
    weight_buf = pl.pallas_call(
        weigh_blocks,
        out_shape=jax.ShapeDtypeStruct((GROUP, ROWS + META, PIX), jnp.bfloat16),
        in_specs=[pl.BlockSpec(memory_space=pltpu.SMEM)] + [HBM_SPEC] * 3,
        out_specs=HBM_SPEC,
        scratch_shapes=[
            pltpu.VMEM((1, HELD), jnp.int32),
            pltpu.VMEM((1, HELD), jnp.int32),
            pltpu.VMEM((META, PIX), jnp.float32),
            pltpu.VMEM((HELD, PIX, PIX), jnp.bfloat16),
            pltpu.VMEM((GROUP, ROWS + META, PIX), jnp.bfloat16),
            pltpu.SemaphoreType.DMA((LOADS + 2,)),
            pltpu.SemaphoreType.DMA((7,)),
        ]
        + scratch * (HELD // BATCH),
        compiler_params=PARAMS,
    )(lax.axis_index("zh").reshape(1), patch_of.reshape(1, HELD), slot_of.reshape(1, HELD), variance)
    group = ("zl", "c", "x", "y")
    weight_got = lax.all_to_all(weight_buf, group, split_axis=0, concat_axis=0, tiled=True)
    matched_buf = pl.pallas_call(
        match_blocks,
        out_shape=jax.ShapeDtypeStruct((GROUP, ROWS, PIX), jnp.bfloat16),
        grid_spec=pltpu.PrefetchScalarGridSpec(
            num_scalar_prefetch=1,
            grid=(HELD // STEP,),
            in_specs=[
                pl.BlockSpec((STEP, PIX, PIX), lambda i, *_: (i, 0, 0)),
                pl.BlockSpec((STEP, PIX, PIX), lambda i, *_: (i, 0, 0)),
                pl.BlockSpec((PIX, 9 * PIX), lambda i, *_: (0, 0)),
                pl.BlockSpec((PIX, 9 * PIX), lambda i, *_: (0, 0)),
            ],
            out_specs=HBM_SPEC,
            scratch_shapes=[pltpu.VMEM((2, 9 * PIX, 2 * PIX), jnp.bfloat16)]
            + scratch
            + [pltpu.VMEM((GROUP, ROWS, PIX), jnp.bfloat16), pltpu.SemaphoreType.DMA((LOADS,))],
        ),
        compiler_params=PARAMS,
        cost_estimate=pl.CostEstimate(flops=6 * 10**9, bytes_accessed=6 * 2**20, transcendentals=0),
    )(coefficients.reshape(-1), images, variance, jnp.asarray(x_table), jnp.asarray(y_table))
    matched_got = lax.all_to_all(matched_buf, group, split_axis=0, concat_axis=0, tiled=True)
    ids, *weight_parts = tile_sums(weight_got)
    depth = pl.pallas_call(
        add_halves,
        out_shape=jax.ShapeDtypeStruct((TILES, 2 * PIX), jnp.float32),
        in_specs=[VMEM_SPEC] * 4,
        out_specs=VMEM_SPEC,
        compiler_params=ADD_PARAMS,
    )(weight_parts[0], *(over_z(weight_parts[by], by) for by in (2, 1, 3)))
    own, up, far, down = tile_sums(matched_got, ids)
    summed = pl.pallas_call(
        add_all,
        out_shape=jax.ShapeDtypeStruct((GROUP, 16, PIX), jnp.bfloat16),
        in_specs=[VMEM_SPEC] * 5,
        out_specs=VMEM_SPEC,
        scratch_shapes=[pltpu.VMEM((GROUP * TURN, PIX), jnp.float32)],
        compiler_params=ADD_PARAMS,
    )(depth, own, over_z(far, 2), over_z(up, 1), over_z(down, 3))
    whole = lax.all_to_all(summed, group, split_axis=0, concat_axis=0, tiled=True)
    out = jax.ShapeDtypeStruct((4, PIX, PIX), jnp.float32)
    return pl.pallas_call(
        combine,
        out_shape=(out, out),
        in_specs=[VMEM_SPEC],
        out_specs=(VMEM_SPEC, VMEM_SPEC),
        scratch_shapes=[pltpu.VMEM((GROUP * TURN, PIX), jnp.float32)],
        compiler_params=ADD_PARAMS,
    )(whole)


def solution(mesh):
    names = ("x", "zh", "zl", "c", "y")
    fine = Mesh(mesh.devices.reshape(4, 4, 2, 2, 4), names)
    return jax.shard_map(
        local,
        mesh=fine,
        in_specs=(P(names, None, None), P(names, None, None), P(names, None, None), P(names, None), P(names)),
        out_specs=(P(names, None, None), P(names, None, None)),
        check_vma=False,
    )
```

```python
import functools

import numpy as np
import ml_dtypes
import jax
import jax.numpy as jnp
from jax import lax
from jax.experimental import pallas as pl
from jax.experimental.pallas import tpu as pltpu
from jax.sharding import Mesh, PartitionSpec as P

PIX = 128
SLOTS = 16
HELD = 48
REACH = 10
GROUP = 64
ROWS = 2 * HELD
META = 16
ALL_BLOCKS = GROUP * HELD
TILES = 256
BATCH = 16
TURN = 24
STRIDE = 40
STEP = 4
LOADS = 8
PARAMS = pltpu.CompilerParams(vmem_limit_bytes=56 * 2**20)
SUM_PARAMS = pltpu.CompilerParams(vmem_limit_bytes=24 * 2**20)
ADD_PARAMS = pltpu.CompilerParams(vmem_limit_bytes=8 * 2**20)

VMEM_SPEC = pl.BlockSpec(memory_space=pltpu.VMEM)
HBM_SPEC = pl.BlockSpec(memory_space=pltpu.HBM)
ANY_SPEC = pl.BlockSpec(memory_space=pl.ANY)


def band(spread, degree):
    t = np.arange(-REACH, REACH + 1)
    scaled = t.astype(np.float32) / np.float32(spread)
    taps = np.exp(np.float32(-0.5) * scaled * scaled) * scaled**degree
    taps = (taps / np.sqrt(np.sum(taps * taps))).astype(np.float32)
    out = np.zeros((PIX, PIX), np.float32)
    for k in range(PIX):
        for off, tap in zip(t, taps):
            if 0 <= k + off < PIX:
                out[k, k + off] = tap
    return out


def tables():
    bands = [band(2.0**s, d) for s in range(3) for d in range(3)]
    x_table = np.concatenate([b.T for b in bands], axis=1).astype(ml_dtypes.bfloat16)
    y_table = np.concatenate(bands, axis=1).astype(ml_dtypes.bfloat16)
    return x_table, y_table


def put(staged, i, value):
    for half in range(2):
        staged[pl.ds(half * BATCH + i % BATCH, GROUP, stride=STRIDE), :] = value[half * GROUP : (half + 1) * GROUP]


def pack(staged, packed, out_hbm, sems, n):
    copies = []
    for half in range(2):
        at = pl.ds(n * BATCH + half * HELD, BATCH)
        for d in range(GROUP):
            row = d * STRIDE + half * BATCH
            packed[d, at, :] = staged[row : row + BATCH, :].astype(jnp.bfloat16)
        copies.append(pltpu.make_async_copy(packed.at[:, at, :], out_hbm.at[:, at, :], sems.at[2 * n + half]))
        copies[-1].start()
    return copies


def weigh_blocks(zh_ref, patch_hbm, slot_hbm, var_hbm, out_hbm, patch_ref, slot_ref, marks, var_ref, packed, in_sems, sems, *staged):
    held = HELD // LOADS
    loads = []
    for n in range(LOADS):
        at = pl.ds(n * held, held)
        loads.append(pltpu.make_async_copy(var_hbm.at[at], var_ref.at[at], in_sems.at[n]))
    loads.append(pltpu.make_async_copy(patch_hbm, patch_ref, in_sems.at[LOADS]))
    loads.append(pltpu.make_async_copy(slot_hbm, slot_ref, in_sems.at[LOADS + 1]))
    for c in loads[-2:] + loads[:-2]:
        c.start()
    for c in loads[-2:]:
        c.wait()
    patch, slot = patch_ref[...], slot_ref[...]
    z_at = (patch // 2) % 8
    z_by = (z_at // 2 + 4 - zh_ref[0]) % 4
    owner = ((z_at % 2 * 2 + patch % 2) * 4 + patch // 16) * 4 + slot // 4
    tile = (z_by * 4 + slot % 4) * GROUP + owner
    low = lax.broadcasted_iota(jnp.int32, (META, HELD), 0) < META // 2
    marks[...] = jnp.zeros_like(marks)
    marks[:, :HELD] = jnp.where(low, tile % PIX, tile // PIX).astype(jnp.float32)
    meta = marks[...].astype(jnp.bfloat16)
    for d in range(GROUP):
        packed[d, ROWS:, :] = meta
    rows = pl.ds(ROWS, META)
    copies = [pltpu.make_async_copy(packed.at[:, rows, :], out_hbm.at[:, rows, :], sems.at[6])]
    copies[0].start()
    for n in range(LOADS):
        loads[n].wait()
        for i in range(n * held, (n + 1) * held):
            put(staged[i // BATCH], i, pl.reciprocal(var_ref[i].astype(jnp.float32), approx=True))
            if i % BATCH == BATCH - 1:
                copies += pack(staged[i // BATCH], packed, out_hbm, sems, i // BATCH)
    for c in copies:
        c.wait()


def match_blocks(coef_ref, img_ref, var_ref, xt_ref, yt_ref, out_hbm, z_ref, staged, packed, sems):
    step = pl.program_id(0)
    last = pl.num_programs(0) - 1

    cols = lax.broadcasted_iota(jnp.int32, (1, PIX), 1).astype(jnp.float32)
    u = (2.0 * cols - (PIX - 1)) / (PIX - 1)
    rows = lax.broadcasted_iota(jnp.int32, (PIX, 1), 0).astype(jnp.float32)
    v = (2.0 * rows - (PIX - 1)) / (PIX - 1)
    for n in range(STEP):
        base = (step * STEP + n) * 45
        x_all = jnp.dot(img_ref[n], xt_ref[...], preferred_element_type=jnp.float32)

        def flat(b):
            return coef_ref[base + b] + coef_ref[base + 15 + b] * u

        def slope(b):
            return coef_ref[base + 30 + b]

        for s in range(3):
            b = 5 * s
            x0, x1, x2 = (x_all[:, (3 * s + d) * PIX : (3 * s + d + 1) * PIX] for d in range(3))
            parts = (
                (flat(b) * x0 + flat(b + 1) * x1 + flat(b + 3) * x2, slope(b) * x0 + slope(b + 1) * x1 + slope(b + 3) * x2),
                (flat(b + 2) * x0, slope(b + 2) * x0),
                (flat(b + 4) * x0, slope(b + 4) * x0),
            )
            for j in range(3):
                k = (3 * s + j) * PIX
                z_ref[n % 2, k : k + PIX, :PIX] = parts[j][0].astype(jnp.bfloat16)
                z_ref[n % 2, k : k + PIX, PIX:] = parts[j][1].astype(jnp.bfloat16)
        both = jnp.dot(yt_ref[...], z_ref[n % 2], preferred_element_type=jnp.float32)
        matched = both[:, :PIX] + v * both[:, PIX:]
        put(staged, step * STEP + n, matched / var_ref[n].astype(jnp.float32))

    each = BATCH // STEP
    for n in range(HELD // BATCH):

        @pl.when(step == (n + 1) * each - 1)
        def _():
            pack(staged, packed, out_hbm, sems, n)

    @pl.when(step == last)
    def _():
        for n in range(HELD // BATCH):
            for half in range(2):
                at = pl.ds(half * HELD + n * BATCH, BATCH)
                pltpu.make_async_copy(packed.at[:, at, :], out_hbm.at[:, at, :], sems.at[2 * n + half]).wait()


def read_marks(got_ref, table, id_ref):
    code = got_ref[:, ROWS:, :].astype(jnp.float32)
    lane = lax.broadcasted_iota(jnp.int32, (GROUP, PIX), 1)
    tile = code[:, 0, :] + PIX * code[:, META // 2, :]
    table[...] = jnp.where(lane < HELD, tile, 0.0).astype(jnp.int32)
    lane = lax.broadcasted_iota(jnp.int32, (8, PIX), 1)
    rows = [jnp.zeros((8, PIX), jnp.int32)] * 4
    for n in range(8):
        row, at = n * HELD // PIX, n * HELD % PIX
        moved = pltpu.roll(table[pl.ds(n, 8, stride=8), :], at, 1) if at else table[pl.ds(n, 8, stride=8), :]
        rows[row] = rows[row] + jnp.where(lane >= at, moved, 0)
        rows[row + 1] = rows[row + 1] + jnp.where(lane < at, moved, 0)
    for row in range(3):
        id_ref[pl.ds(row, 8, stride=3), :] = rows[row]


def sum_blocks(id_ref, got_ref, outs, hot):
    tile = lax.broadcasted_iota(jnp.int32, (4 * TILES, PIX), 0)
    for k in range(ALL_BLOCKS // PIX):
        hot[:, k * PIX : (k + 1) * PIX] = (id_ref[k : k + 1, :] == tile).astype(jnp.bfloat16)
    halves = [got_ref[:, half * HELD : (half + 1) * HELD, :].reshape(ALL_BLOCKS, PIX) for half in range(2)]
    total = jnp.dot(hot[...], jnp.concatenate(halves, axis=1), preferred_element_type=jnp.float32).astype(jnp.bfloat16)
    for m, out in enumerate(outs):
        out[...] = total[m * TILES : (m + 1) * TILES]


def sum_weights(got_ref, id_ref, *refs):
    read_marks(got_ref, refs[5], id_ref)
    sum_blocks(id_ref, got_ref, refs[:4], refs[4])


def sum_matched(id_ref, got_ref, *refs):
    sum_blocks(id_ref, got_ref, refs[:4], refs[4])


def tile_sums(got, ids=None):
    part = jax.ShapeDtypeStruct((TILES, 2 * PIX), jnp.bfloat16)
    hot = pltpu.VMEM((4 * TILES, ALL_BLOCKS), jnp.bfloat16)
    if ids is not None:
        return pl.pallas_call(
            sum_matched,
            out_shape=[part] * 4,
            in_specs=[VMEM_SPEC] * 2,
            out_specs=[VMEM_SPEC] * 4,
            scratch_shapes=[hot],
            compiler_params=SUM_PARAMS,
        )(ids, got)
    return pl.pallas_call(
        sum_weights,
        out_shape=[jax.ShapeDtypeStruct((ALL_BLOCKS // PIX, PIX), jnp.int32)] + [part] * 4,
        in_specs=[VMEM_SPEC],
        out_specs=[VMEM_SPEC] * 5,
        scratch_shapes=[hot, pltpu.VMEM((GROUP, PIX), jnp.int32)],
        compiler_params=SUM_PARAMS,
    )(got)


def over_z(part, by):
    return lax.ppermute(part, "zh", [(i, (i + by) % 4) for i in range(4)])


def add_halves(a_ref, b_ref, c_ref, d_ref, out_ref):
    out_ref[...] = sum(ref[...].astype(jnp.float32) for ref in (a_ref, b_ref, c_ref, d_ref))


def add_all(depth_ref, a_ref, b_ref, c_ref, d_ref, out_ref, turned):
    num = sum(ref[...].astype(jnp.float32) for ref in (a_ref, b_ref, c_ref, d_ref))
    for n, total in enumerate((depth_ref[...], num)):
        for half in range(2):
            for s in range(4):
                at = pl.ds((2 * n + half) * 4 + s, GROUP, stride=TURN)
                turned[at, :] = total[s * GROUP : (s + 1) * GROUP, half * PIX : (half + 1) * PIX]
    for d in range(GROUP):
        out_ref[d] = turned[d * TURN : d * TURN + 16, :].astype(jnp.bfloat16)


def combine(got_ref, coadd_ref, depth_ref, flat):
    for d in range(GROUP):
        flat[d * TURN : d * TURN + 16, :] = got_ref[d].astype(jnp.float32)
    for s in range(4):
        for half in range(2):
            rows = slice(half * GROUP, (half + 1) * GROUP)
            depth = flat[pl.ds(half * 4 + s, GROUP, stride=TURN), :]
            num = flat[pl.ds((2 + half) * 4 + s, GROUP, stride=TURN), :]
            depth_ref[s, rows, :] = depth
            coadd_ref[s, rows, :] = num / jnp.maximum(depth, 1.0)


def local(images, variance, coefficients, patch_of, slot_of):
    x_table, y_table = tables()
    scratch = [pltpu.VMEM((GROUP * STRIDE, PIX), jnp.float32)]
    weight_buf = pl.pallas_call(
        weigh_blocks,
        out_shape=jax.ShapeDtypeStruct((GROUP, ROWS + META, PIX), jnp.bfloat16),
        in_specs=[pl.BlockSpec(memory_space=pltpu.SMEM)] + [HBM_SPEC] * 3,
        out_specs=HBM_SPEC,
        scratch_shapes=[
            pltpu.VMEM((1, HELD), jnp.int32),
            pltpu.VMEM((1, HELD), jnp.int32),
            pltpu.VMEM((META, PIX), jnp.float32),
            pltpu.VMEM((HELD, PIX, PIX), jnp.bfloat16),
            pltpu.VMEM((GROUP, ROWS + META, PIX), jnp.bfloat16),
            pltpu.SemaphoreType.DMA((LOADS + 2,)),
            pltpu.SemaphoreType.DMA((7,)),
        ]
        + scratch * (HELD // BATCH),
        compiler_params=PARAMS,
    )(lax.axis_index("zh").reshape(1), patch_of.reshape(1, HELD), slot_of.reshape(1, HELD), variance)
    group = ("zl", "c", "x", "y")
    weight_got = lax.all_to_all(weight_buf, group, split_axis=0, concat_axis=0, tiled=True)
    matched_buf = pl.pallas_call(
        match_blocks,
        out_shape=jax.ShapeDtypeStruct((GROUP, ROWS, PIX), jnp.bfloat16),
        grid_spec=pltpu.PrefetchScalarGridSpec(
            num_scalar_prefetch=1,
            grid=(HELD // STEP,),
            in_specs=[
                pl.BlockSpec((STEP, PIX, PIX), lambda i, *_: (i, 0, 0)),
                pl.BlockSpec((STEP, PIX, PIX), lambda i, *_: (i, 0, 0)),
                pl.BlockSpec((PIX, 9 * PIX), lambda i, *_: (0, 0)),
                pl.BlockSpec((PIX, 9 * PIX), lambda i, *_: (0, 0)),
            ],
            out_specs=HBM_SPEC,
            scratch_shapes=[pltpu.VMEM((2, 9 * PIX, 2 * PIX), jnp.bfloat16)]
            + scratch
            + [pltpu.VMEM((GROUP, ROWS, PIX), jnp.bfloat16), pltpu.SemaphoreType.DMA((LOADS,))],
        ),
        compiler_params=PARAMS,
        cost_estimate=pl.CostEstimate(flops=6 * 10**9, bytes_accessed=6 * 2**20, transcendentals=0),
    )(coefficients.reshape(-1), images, variance, jnp.asarray(x_table), jnp.asarray(y_table))
    matched_got = lax.all_to_all(matched_buf, group, split_axis=0, concat_axis=0, tiled=True)
    ids, *weight_parts = tile_sums(weight_got)
    depth = pl.pallas_call(
        add_halves,
        out_shape=jax.ShapeDtypeStruct((TILES, 2 * PIX), jnp.float32),
        in_specs=[VMEM_SPEC] * 4,
        out_specs=VMEM_SPEC,
        compiler_params=ADD_PARAMS,
    )(weight_parts[0], *(over_z(weight_parts[by], by) for by in (2, 1, 3)))
    own, up, far, down = tile_sums(matched_got, ids)
    summed = pl.pallas_call(
        add_all,
        out_shape=jax.ShapeDtypeStruct((GROUP, 16, PIX), jnp.bfloat16),
        in_specs=[VMEM_SPEC] * 5,
        out_specs=VMEM_SPEC,
        scratch_shapes=[pltpu.VMEM((GROUP * TURN, PIX), jnp.float32)],
        compiler_params=ADD_PARAMS,
    )(depth, own, over_z(far, 2), over_z(up, 1), over_z(down, 3))
    whole = lax.all_to_all(summed, group, split_axis=0, concat_axis=0, tiled=True)
    out = jax.ShapeDtypeStruct((4, PIX, PIX), jnp.float32)
    return pl.pallas_call(
        combine,
        out_shape=(out, out),
        in_specs=[VMEM_SPEC],
        out_specs=(VMEM_SPEC, VMEM_SPEC),
        scratch_shapes=[pltpu.VMEM((GROUP * TURN, PIX), jnp.float32)],
        compiler_params=ADD_PARAMS,
    )(whole)


def solution(mesh):
    names = ("x", "zh", "zl", "c", "y")
    fine = Mesh(mesh.devices.reshape(4, 4, 2, 2, 4), names)
    return jax.shard_map(
        local,
        mesh=fine,
        in_specs=(P(names, None, None), P(names, None, None), P(names, None, None), P(names, None), P(names)),
        out_specs=(P(names, None, None), P(names, None, None)),
        check_vma=False,
    )
```
